768 devices in a mesh: src: 8 (over y), dst: 96 (over z, x, core).
Axes of the slice: x: 4, y: 8, z: 12, core: 2. Of those that a mesh axis runs over, the one named last changes fastest.
Arguments:
- node_feats: bfloat16 [12288, 256], P(('dst', 'src')), may hold values from -6 to 6
- cotangent: bfloat16 [12288, 256], P(('src', 'dst')), may hold values from -6 to 6
- edge_attr: bfloat16 [1179648, 128], P(('src', 'dst')), may hold values from -6 to 6
- src_ids: int32 [1179648], P(('src', 'dst')), may hold values from 0 to 127
- dst_rel: int32 [1179648], P(('src', 'dst')), may hold values from 0 to 127
- offsets: int32 [9216], P(('src', 'dst')), may hold values from 0 to 1408
- counts: int32 [9216], P(('src', 'dst')), may hold values from 32 to 128
- w_node: bfloat16 [256, 512], replicated, may hold values from -0.375 to 0.375
- w_edge: bfloat16 [128, 512], replicated, may hold values from -0.5 to 0.5
- bias: float32 [512], replicated, may hold values from -3 to 3
- w_out: bfloat16 [512, 256], replicated, may hold values from -0.03125 to 0.03125
Outputs:
- aggregated: bfloat16 [12288, 256], P(('src', 'dst'))
- node_grads: bfloat16 [12288, 256], P(('dst', 'src'))
- attr_grads: bfloat16 [1179648, 128], P(('src', 'dst'))
The draws below stay inside these ranges and needn't reach their ends.
Inputs may be any that keep to these rules, and one draw needn't show every extreme that they name: `counts`: slots at or after a block's count carry no edge; their ids are arbitrary within range.
All inputs are finite; a program needn't handle non-finite values.
Results may differ from the reference program's by a relative error of at most 0.0049.
Values may be sent and summed in bfloat16 or wider, within the bound.
A program may use at most 32 MiB of HBM per device.

```python
import jax
import jax.numpy as jnp
from jax import lax

W = 256
H = 512
EF = 128
BLOCK = 128
NODE_DEV = 16
BLK_DEV = 12
NODES = 12288
BLOCKS = 9216
EDGES = 1179648
N_SRC = 8
N_DST = 96


def place_ends(result, own_key, least, high):
    longest = result.shape.index(max(result.shape))
    spots = []
    for shift in (0, 1):
        where = [jax.random.randint(jax.random.fold_in(own_key, axis), (), 0, length) for axis, length in enumerate(result.shape)]
        where[longest] = (where[longest] + shift) % result.shape[longest]
        spots.append(tuple(where))
    return result.at[spots[0]].set(least).at[spots[1]].set(high)


def shard_levels(rng, shape, shards, low, largest):
    loudness = 1.0
    for axis_at, blocks in shards:
        heights = jax.random.uniform(jax.random.fold_in(jax.random.fold_in(rng, 6), axis_at), (blocks,), jnp.float32, low / len(shards), largest / len(shards))
        loudness = loudness * jnp.repeat(jnp.exp(heights), shape[axis_at] // blocks).reshape((-1,) + (1,) * (len(shape) - 1 - axis_at))
    return loudness


def noise(rng, dims, spread, bound, cuts=(), kind=jnp.bfloat16):
    factor_of = shard_levels(rng, dims, cuts, -0.22, 0.18) if cuts else 1.0
    array = jax.random.normal(rng, dims, jnp.float32) * spread * factor_of
    return jnp.minimum(jnp.maximum(array, -bound), bound).astype(kind)


def setup_inputs(seed: int = 0) -> dict:
    seeds = jax.random.split(jax.random.key(seed), 12)
    node_feats = noise(seeds[0], (NODES, W), 1.0, 6.0, ((0, 768),))
    cotangent = noise(seeds[1], (NODES, W), 1.0, 6.0, ((0, 768),))
    edge_attr = noise(seeds[2], (EDGES, EF), 1.0, 6.0, ((0, 768),))
    src_ids = place_ends(jax.random.randint(seeds[3], (EDGES,), 0, NODE_DEV * N_SRC), jax.random.fold_in(seeds[3], 1), 0, (NODE_DEV * N_SRC) - 1).astype(jnp.int32)
    dst_rel = place_ends(jax.random.randint(seeds[4], (EDGES,), 0, BLOCK), jax.random.fold_in(seeds[4], 1), 0, BLOCK - 1).astype(jnp.int32)
    offsets = place_ends(jax.random.randint(seeds[5], (BLOCKS,), 0, NODE_DEV * N_DST - BLOCK + 1), jax.random.fold_in(seeds[5], 1), 0, NODE_DEV * N_DST - BLOCK).astype(jnp.int32)
    counts = place_ends(jax.random.randint(seeds[6], (BLOCKS,), 32, BLOCK + 1), jax.random.fold_in(seeds[6], 1), 32, BLOCK).astype(jnp.int32)
    w_node = noise(seeds[7], (W, H), W ** -0.5, 0.375)
    w_edge = noise(seeds[8], (EF, H), EF ** -0.5, 0.5)
    bias = noise(seeds[9], (H,), 0.5, 3.0, (), jnp.float32)
    w_out = noise(seeds[10], (H, W), (H * 64) ** -0.5, 0.03125)
    return {"node_feats": node_feats, "cotangent": cotangent, "edge_attr": edge_attr, "src_ids": src_ids, "dst_rel": dst_rel, "offsets": offsets, "counts": counts, "w_node": w_node, "w_edge": w_edge, "bias": bias, "w_out": w_out}


def reference(node_feats, cotangent, edge_attr, src_ids, dst_rel, offsets, counts, w_node, w_edge, bias, w_out):
    devs = N_SRC * N_DST
    per = BLK_DEV * BLOCK
    src_all = src_ids.reshape(devs, per)
    rel_all = dst_rel.reshape(devs, BLK_DEV, BLOCK)
    off_all = offsets.reshape(devs, BLK_DEV)
    cnt_all = counts.reshape(devs, BLK_DEV)
    attr_all = edge_attr.reshape(devs, per, EF)
    index_all = jnp.arange(devs, dtype=jnp.int32)

    def one(carry, items):
        agg, grads = carry
        src_k, rel_k, off_k, cnt_k, attr_k, k = items
        s_part = k // N_DST
        d_part = k % N_DST
        slots = lax.broadcasted_iota(jnp.int32, (BLK_DEV, BLOCK), 1)
        valid = (slots < cnt_k[:, None]).reshape(per)
        source = (d_part * (N_SRC * NODE_DEV) + src_k).astype(jnp.int32)
        target = (s_part * (N_DST * NODE_DEV) + off_k[:, None] + rel_k).reshape(per).astype(jnp.int32)
        x_e = node_feats[source]
        pre = jnp.dot(x_e, w_node, preferred_element_type=jnp.float32) + jnp.dot(attr_k, w_edge, preferred_element_type=jnp.float32) + bias
        hidden = jax.nn.silu(pre).astype(jnp.bfloat16)
        message = jnp.dot(hidden, w_out, preferred_element_type=jnp.float32)
        message = jnp.where(valid[:, None], message, jnp.float32(0.0))
        agg = agg.at[target].add(message)
        d_message = jnp.where(valid[:, None], cotangent[target], jnp.bfloat16(0.0)).astype(jnp.bfloat16)
        d_hidden = jnp.dot(d_message, w_out.T, preferred_element_type=jnp.float32)
        sig = jax.nn.sigmoid(pre)
        d_pre = (d_hidden * sig * (1.0 + pre * (1.0 - sig))).astype(jnp.bfloat16)
        d_attr = jnp.dot(d_pre, w_edge.T, preferred_element_type=jnp.float32).astype(jnp.bfloat16)
        d_source = jnp.dot(d_pre, w_node.T, preferred_element_type=jnp.float32)
        grads = grads.at[source].add(d_source)
        return (agg, grads), d_attr

    start = (jnp.zeros((NODES, W), jnp.float32), jnp.zeros((NODES, W), jnp.float32))
    (agg, grads), d_attrs = lax.scan(one, start, (src_all, rel_all, off_all, cnt_all, attr_all, index_all))
    return agg.astype(jnp.bfloat16), grads.astype(jnp.bfloat16), d_attrs.reshape(EDGES, EF)
```

```python
import functools

import jax
import jax.numpy as jnp
from jax import lax
from jax.experimental import pallas as pl
from jax.experimental.pallas import tpu as pltpu
from jax.sharding import PartitionSpec as P

MESH = pl.DeviceIdType.MESH
X_CHIPS = 4
CORES = 2
WINDOW = 256
NT = (((1,), (1,)), ((), ()))


def split_bf16(value):
    high = value.astype(jnp.bfloat16)
    low = (value - high.astype(jnp.float32)).astype(jnp.bfloat16)
    return high, low


def kernel(
    dims,
    feats_in, cot_in, attr_in, src_in, rel_in, offsets, counts, wnode_in, wedge_in, bias_in, wout_in,
    agg_out, node_out, attr_out,
    group, cot, attr, src, rel, wnode, wedge, bias, wout,
    hot_src, hot_src_t, hot_dst, hot_win,
    proj, pre, msg, dpre, attr_grad,
    half_out, half_in, own, x_out, x_in, z_out, z_in, s_out, s_in, agg, node,
    load_sem, feat_send, feat_recv, cx_send, cx_recv, cz_send, cz_recv, cc_send, cc_recv,
    half_send, half_recv, x_send, x_recv, z_send, z_recv, s_send, s_recv, store_sem,
):
    n_src, n_x, n_z, rows = dims
    blocks, width = src.shape
    edges = blocks * width
    feat = group.shape[2]
    me_s = lax.axis_index("src")
    me_d = lax.axis_index("dst")
    me_c = lax.rem(me_d, CORES)
    me_x = lax.rem(lax.div(me_d, CORES), n_x)
    me_z = lax.div(me_d, CORES * n_x)
    slab = rows * n_z
    half = slab * n_x

    def dst_at(z, x, c):
        return (z * n_x + x) * CORES + c

    def y_peer(k):
        return (lax.rem(me_s + k, n_src), me_d)

    def x_peer(k):
        return (me_s, dst_at(me_z, lax.rem(me_x + k, n_x), me_c))

    def z_peer(k):
        return (me_s, dst_at(lax.rem(me_z + k, n_z), me_x, me_c))

    sibling = (me_s, dst_at(me_z, me_x, 1 - me_c))

    def remote(source, target, send, recv, device):
        return pltpu.make_async_remote_copy(
            src_ref=source, dst_ref=target, send_sem=send, recv_sem=recv,
            device_id=device, device_id_type=MESH,
        )

    def loop(first, last, step):
        def body(k, carry):
            step(k)
            return carry
        lax.fori_loop(first, last, body, 0)

    loads = [
        pltpu.make_async_copy(source, target, load_sem.at[i])
        for i, (source, target) in enumerate(
            (
                (src_in, src), (rel_in, rel), (attr_in, attr), (wedge_in, wedge), (bias_in, bias),
                (wnode_in, wnode), (wout_in, wout),
                (feats_in, group.at[me_s]), (cot_in, cot.at[me_z * n_x + me_x, me_c]),
            )
        )
    ]
    for load in loads:
        load.start()

    barrier = pltpu.get_barrier_semaphore()

    def greet(device):
        pl.semaphore_signal(barrier, inc=1, device_id=device, device_id_type=MESH)

    loop(1, n_src, lambda k: greet(y_peer(k)))
    loop(1, n_x, lambda k: greet(x_peer(k)))
    loop(1, n_z, lambda k: greet(z_peer(k)))
    greet(sibling)
    pl.semaphore_wait(barrier, n_src + n_x + n_z - 2)

    def feat_copy(k):
        return remote(feats_in, group.at[me_s], feat_send.at[k], feat_recv.at[k], y_peer(k))

    def cx_copy(k):
        return remote(
            cot_in, cot.at[me_z * n_x + me_x, me_c], cx_send.at[k], cx_recv.at[k], x_peer(k)
        )

    loop(1, n_src, lambda k: feat_copy(k).start())
    loop(1, n_x, lambda k: cx_copy(k).start())

    def own_slab(z):
        return cot.at[pl.ds(z * n_x, n_x), me_c]

    def cz_copy(k):
        return remote(own_slab(me_z), own_slab(me_z), cz_send.at[k], cz_recv.at[k], z_peer(k))

    def cc_copy(k):
        z = lax.rem(me_z + n_z - k, n_z)
        return remote(own_slab(z), own_slab(z), cc_send.at[k], cc_recv.at[k], sibling)

    loads[0].wait()
    loads[1].wait()
    lane = lax.broadcasted_iota(jnp.int32, (width, width), 1)
    sub = lax.broadcasted_iota(jnp.int32, (width, width), 0)
    tall = lax.broadcasted_iota(jnp.int32, (CORES * half, width), 0)
    one_lane = lax.broadcasted_iota(jnp.int32, (1, width), 1)

    def hot(mask):
        return jnp.where(mask, 1.0, 0.0).astype(jnp.bfloat16)

    def mark(b):
        at = pl.multiple_of(b * width, width)
        here = pl.ds(at, width)
        ids = src[pl.ds(b, 1), :]
        picked = hot(jnp.broadcast_to(ids, (width, width)).T == lane)
        hot_src[here, 0:width] = picked
        hot_src[here, width : 2 * width] = picked
        owner = lax.rem((ids >> 4) + (n_src - me_s), n_src)
        hot_src_t[:, here] = hot(sub[: n_src * rows] == owner * rows + (ids & (rows - 1)))
        valid = one_lane < counts[b]
        start = offsets[b]
        target = rel[pl.ds(b, 1), :] + start
        peer = target >> 4
        core = lax.rem(peer + me_c, CORES)
        x = lax.rem((peer >> 1) + (n_x - me_x), n_x)
        z = lax.rem(lax.div(peer, CORES * n_x) + (n_z - me_z), n_z)
        place = ((core * n_x + x) * n_z + z) * rows + (target & (rows - 1))
        hot_dst[:, here] = hot(tall == jnp.where(valid, place, -1))
        base = jnp.minimum(start >> 5, cot.shape[0] - WINDOW // (CORES * rows)) * (CORES * rows)
        inside = jnp.broadcast_to(jnp.where(valid, target - base, -1), (width, width)).T
        hot_win[here, 0:width] = hot(inside == lane)
        hot_win[here, width : 2 * width] = hot(inside == lane + width)

    loop(0, blocks, mark)

    for i in (2, 3, 4):
        loads[i].wait()
    tile = min(256, edges)

    def attr_part(i):
        here = pl.ds(pl.multiple_of(i * tile, tile), tile)
        pre[here, :] = (
            jnp.dot(attr[here, :], wedge[...], preferred_element_type=jnp.float32) + bias[...]
        )

    loop(0, edges // tile, attr_part)

    loads[8].wait()
    loop(1, n_x, lambda k: cx_copy(k).wait_recv())
    loop(1, n_z, lambda k: cz_copy(k).start())
    cc_copy(0).start()

    loads[5].wait()
    loads[6].wait()
    loads[7].wait()
    loop(1, n_src, lambda k: feat_copy(k).wait_recv())
    high, low = split_bf16(
        jnp.dot(
            group[...].reshape(n_src * rows, feat), wnode[...], preferred_element_type=jnp.float32
        )
    )
    if n_src * rows < width:
        proj[...] = jnp.zeros_like(proj)
    proj[0 : n_src * rows, :] = high
    proj[width : width + n_src * rows, :] = low

    def forward(i):
        here = pl.ds(pl.multiple_of(i * tile, tile), tile)
        value = pre[here, :] + jnp.dot(
            hot_src[here, :], proj[...], preferred_element_type=jnp.float32
        )
        sig = 0.5 * jnp.tanh(0.5 * value) + 0.5
        hidden = (value * sig).astype(jnp.bfloat16)
        pre[here, :] = sig * (1.0 + value * (1.0 - sig))
        msg[here, :] = jnp.dot(hidden, wout[...], preferred_element_type=jnp.float32).astype(
            jnp.bfloat16
        )

    loop(0, edges // tile, forward)

    def half_copy(k):
        part = pl.ds(k * slab, slab)
        return remote(
            half_out.at[part], half_in.at[part], half_send.at[k], half_recv.at[k], sibling
        )

    def x_copy(k):
        return remote(
            x_out.at[k - 1], x_in.at[k - 1], x_send.at[k - 1], x_recv.at[k - 1], x_peer(k)
        )

    order = tuple(range(1, n_x)) + (0,)
    for k in order:
        half_out[k * slab : (k + 1) * slab, :] = jnp.dot(
            hot_dst[half + k * slab : half + (k + 1) * slab, :],
            msg[...],
            preferred_element_type=jnp.float32,
        )
        half_copy(k).start()
    for k in order:
        total = jnp.dot(
            hot_dst[k * slab : (k + 1) * slab, :], msg[...], preferred_element_type=jnp.float32
        )
        half_copy(k).wait_recv()
        total = total + half_in[k * slab : (k + 1) * slab, :]
        if k:
            x_out[k - 1] = total.astype(jnp.bfloat16)
            x_copy(k).start()
        else:
            own[...] = total

    def z_copy(k):
        return remote(
            z_out.at[k - 1], z_in.at[k - 1], z_send.at[k - 1], z_recv.at[k - 1], z_peer(k)
        )

    for k in range(1, n_x):
        x_copy(k).wait_recv()
    summed = own[...]
    for k in range(1, n_x):
        summed = summed + x_in[k - 1].astype(jnp.float32)
    own[...] = summed
    z_out[...] = summed[rows:].astype(jnp.bfloat16).reshape(n_z - 1, rows, feat)
    loop(1, n_z, lambda k: z_copy(k).start())

    def pass_on(k):
        cz_copy(k).wait_recv()
        cc_copy(k).start()

    loop(1, n_z, pass_on)
    loop(0, n_z, lambda k: cc_copy(k).wait_recv())

    def backward(b):
        here = pl.ds(pl.multiple_of(b * width, width), width)
        first = jnp.minimum(offsets[b] >> 5, cot.shape[0] - WINDOW // (CORES * rows))
        window = cot[pl.ds(first, WINDOW // (CORES * rows))].reshape(WINDOW, feat)
        d_message = jnp.dot(
            hot_win[here, :], window, preferred_element_type=jnp.float32
        ).astype(jnp.bfloat16)
        d_hidden = lax.dot_general(d_message, wout[...], NT, preferred_element_type=jnp.float32)
        d_pre = (d_hidden * pre[here, :]).astype(jnp.bfloat16)
        dpre[here, :] = d_pre
        attr_grad[here, :] = lax.dot_general(
            d_pre, wedge[...], NT, preferred_element_type=jnp.float32
        ).astype(jnp.bfloat16)

    loop(0, blocks, backward)
    attr_store = pltpu.make_async_copy(attr_grad, attr_out, store_sem.at[0])
    attr_store.start()
    high, low = split_bf16(
        jnp.dot(hot_src_t[...], dpre[...], preferred_element_type=jnp.float32)
    )
    sums = lax.dot_general(
        high, wnode[...], NT, preferred_element_type=jnp.float32
    ) + lax.dot_general(low, wnode[...], NT, preferred_element_type=jnp.float32)
    s_out[...] = sums.reshape(n_src, rows, feat)

    def s_copy(k):
        return remote(s_out.at[k], s_in.at[k - 1], s_send.at[k - 1], s_recv.at[k - 1], y_peer(k))

    loop(1, n_src, lambda k: s_copy(k).start())

    loop(1, n_z, lambda k: z_copy(k).wait_recv())
    agg[...] = (own[0:rows, :] + jnp.sum(z_in[...].astype(jnp.float32), axis=0)).astype(jnp.bfloat16)
    agg_store = pltpu.make_async_copy(agg, agg_out, store_sem.at[1])
    agg_store.start()
    loop(1, n_src, lambda k: s_copy(k).wait_recv())
    node[...] = (s_out[0] + jnp.sum(s_in[...], axis=0)).astype(jnp.bfloat16)
    node_store = pltpu.make_async_copy(node, node_out, store_sem.at[2])
    node_store.start()

    loop(1, n_src, lambda k: feat_copy(k).wait_send())
    loop(1, n_x, lambda k: cx_copy(k).wait_send())
    loop(1, n_z, lambda k: cz_copy(k).wait_send())
    loop(0, n_z, lambda k: cc_copy(k).wait_send())
    for k in range(n_x):
        half_copy(k).wait_send()
    for k in range(1, n_x):
        x_copy(k).wait_send()
    loop(1, n_z, lambda k: z_copy(k).wait_send())
    loop(1, n_src, lambda k: s_copy(k).wait_send())
    attr_store.wait()
    agg_store.wait()
    node_store.wait()


def local(
    n_src, n_x, n_z,
    node_feats, cotangent, edge_attr, src_ids, dst_rel, offsets, counts, w_node, w_edge, bias, w_out,
):
    rows, feat = node_feats.shape
    edges, attr_width = edge_attr.shape
    blocks = offsets.shape[0]
    width = edges // blocks
    hidden = w_node.shape[1]
    slab = rows * n_z
    half = slab * n_x
    f32, bf16 = jnp.float32, jnp.bfloat16
    vmem, dma = pltpu.VMEM, pltpu.SemaphoreType.DMA
    anywhere = pl.BlockSpec(memory_space=pl.ANY)
    scalars = pl.BlockSpec(memory_space=pltpu.SMEM)
    return pl.pallas_call(
        functools.partial(kernel, (n_src, n_x, n_z, rows)),
        out_shape=(
            jax.ShapeDtypeStruct((rows, feat), bf16),
            jax.ShapeDtypeStruct((rows, feat), bf16),
            jax.ShapeDtypeStruct((edges, attr_width), bf16),
        ),
        in_specs=[anywhere] * 5 + [scalars] * 2 + [anywhere] * 4,
        out_specs=(anywhere,) * 3,
        scratch_shapes=[
            vmem((n_src, rows, feat), bf16),
            vmem((n_z * n_x, CORES, rows, feat), bf16),
            vmem((edges, attr_width), bf16),
            vmem((blocks, width), jnp.int32),
            vmem((blocks, width), jnp.int32),
            vmem(w_node.shape, bf16),
            vmem(w_edge.shape, bf16),
            vmem((1, hidden), f32),
            vmem(w_out.shape, bf16),
            vmem((edges, 2 * width), bf16),
            vmem((n_src * rows, edges), bf16),
            vmem((CORES * half, edges), bf16),
            vmem((edges, WINDOW), bf16),
            vmem((2 * width, hidden), bf16),
            vmem((edges, hidden), f32),
            vmem((edges, feat), bf16),
            vmem((edges, hidden), bf16),
            vmem((edges, attr_width), bf16),
            vmem((half, feat), f32),
            vmem((half, feat), f32),
            vmem((slab, feat), f32),
            vmem((n_x - 1, slab, feat), bf16),
            vmem((n_x - 1, slab, feat), bf16),
            vmem((n_z - 1, rows, feat), bf16),
            vmem((n_z - 1, rows, feat), bf16),
            vmem((n_src, rows, feat), f32),
            vmem((n_src - 1, rows, feat), f32),
            vmem((rows, feat), bf16),
            vmem((rows, feat), bf16),
            dma((9,)),
            dma((n_src,)),
            dma((n_src,)),
            dma((n_x,)),
            dma((n_x,)),
            dma((n_z,)),
            dma((n_z,)),
            dma((n_z,)),
            dma((n_z,)),
            dma((n_x,)),
            dma((n_x,)),
            dma((n_x - 1,)),
            dma((n_x - 1,)),
            dma((n_z - 1,)),
            dma((n_z - 1,)),
            dma((n_src - 1,)),
            dma((n_src - 1,)),
            dma((3,)),
        ],
        compiler_params=pltpu.CompilerParams(
            collective_id=0, has_side_effects=True, vmem_limit_bytes=48 * 1024 * 1024
        ),
    )(
        node_feats, cotangent, edge_attr,
        src_ids.reshape(blocks, width), dst_rel.reshape(blocks, width), offsets, counts,
        w_node, w_edge, bias.reshape(1, hidden), w_out,
    )


def build(mesh, n_x):
    n_src, n_dst = mesh.shape["src"], mesh.shape["dst"]
    in_specs = (
        P(("dst", "src"), None),
        P(("src", "dst"), None),
        P(("src", "dst"), None),
        P(("src", "dst")),
        P(("src", "dst")),
        P(("src", "dst")),
        P(("src", "dst")),
        P(),
        P(),
        P(),
        P(),
    )
    out_specs = (P(("src", "dst"), None), P(("dst", "src"), None), P(("src", "dst"), None))
    return jax.shard_map(
        functools.partial(local, n_src, n_x, n_dst // (n_x * CORES)),
        mesh=mesh, in_specs=in_specs, out_specs=out_specs, check_vma=False,
    )


def solution(mesh):
    return build(mesh, X_CHIPS)
```

```python
import functools

import jax
import jax.numpy as jnp
from jax import lax
from jax.experimental import pallas as pl
from jax.experimental.pallas import tpu as pltpu
from jax.sharding import PartitionSpec as P

MESH = pl.DeviceIdType.MESH
X_CHIPS = 4
CORES = 2
WINDOW = 256
NT = (((1,), (1,)), ((), ()))


def split_bf16(value):
    high = value.astype(jnp.bfloat16)
    low = (value - high.astype(jnp.float32)).astype(jnp.bfloat16)
    return high, low


def loop(first, last, step, unroll=1):
    def body(k, carry):
        step(k)
        return carry

    lax.fori_loop(first, last, body, 0, unroll=unroll)


def far_first(size, step, first=0, last=None):
    def body(i):
        step(size // 2 + (1 - 2 * lax.rem(i, 2)) * lax.div(i + 1, 2))

    loop(first, size - 1 if last is None else last, body)


def kernel(
    dims,
    feats_in, cot_in, attr_in, src_in, rel_in, offsets_in, counts_in, wnode_in, wedge_in, bias_in,
    wout_in,
    agg_out, node_out, attr_out,
    offsets, counts, group, cot, attr, src, rel, wnode, wedge, bias, wout,
    hot_src, hot_src_t, hot_dst, hot_win,
    proj, pre, msg, dpre, attr_grad,
    half_out, half_in, kept, own, far, x_out, x_in, b_out, b_in, far_out, far_in, z_out, z_in, s_out, s_in,
    agg, node,
    load_sem, half_recv, store_sem,
    feat_send, feat_recv, cot_send, cot_recv, cz_send, cz_recv, relay_send, relay_recv, cc_send, cc_recv, half_send,
    x_send, x_recv, b_send, b_recv, far_send, far_recv, z_send, z_recv, s_send, s_recv,
):
    n_src, n_x, n_z, rows = dims
    blocks, width = src.shape
    edges = blocks * width
    feat = group.shape[2]
    me_s = lax.axis_index("src")
    me_d = lax.axis_index("dst")
    me_c = lax.rem(me_d, CORES)
    me_x = lax.rem(lax.div(me_d, CORES), n_x)
    me_z = lax.div(me_d, CORES * n_x)
    slab = rows * n_z
    half = slab * n_x
    across = n_x // 2

    def dst_at(z, x, c):
        return (z * n_x + x) * CORES + c

    def y_peer(k):
        return (lax.rem(me_s + k, n_src), me_d)

    def peer(z, x):
        return (
            me_s, dst_at(lax.rem(me_z + z + n_z, n_z), lax.rem(me_x + x + n_x, n_x), me_c),
        )

    sibling = (me_s, dst_at(me_z, me_x, 1 - me_c))

    def remote(source, target, send, recv, device):
        return pltpu.make_async_remote_copy(
            src_ref=source, dst_ref=target, send_sem=send.at[0], recv_sem=recv,
            device_id=device, device_id_type=MESH,
        )

    def all_of(ref, send, recv):
        return remote(ref, ref, send, recv.at[0], sibling)


    with jax.named_scope("load"):
        loads = [
            pltpu.make_async_copy(source, target, load_sem.at[i])
            for i, (source, target) in enumerate(
                (
                    (feats_in, group.at[me_s]), (cot_in, cot.at[me_z * n_x + me_x, me_c]),
                    (src_in, src), (rel_in, rel), (offsets_in, offsets), (counts_in, counts),
                    (attr_in, attr), (wedge_in, wedge), (bias_in, bias),
                    (wnode_in, wnode), (wout_in, wout),
                )
            )
        ]
        for load in loads:
            load.start()

    with jax.named_scope("barrier"):
        barrier = pltpu.get_barrier_semaphore()

        def greet(device):
            pl.semaphore_signal(barrier, inc=1, device_id=device, device_id_type=MESH)

        far_first(n_src, lambda k: greet(y_peer(k)))
        far_first(n_z, lambda k: greet(peer(k, 0)))
        for k in range(1, n_x):
            greet(peer(0, k))
        greet(sibling)
        loads[0].wait()
        loads[1].wait()
        pl.semaphore_wait(barrier, (n_src - 1) + (n_z - 1) + (n_x - 1) + 1)

    with jax.named_scope("first_sends"):
        mine = group.at[me_s]
        far_first(
            n_src, lambda k: remote(mine, mine, feat_send, feat_recv.at[0], y_peer(k)).start()
        )

        def cot_at(z, x):
            return cot.at[z * n_x + lax.rem(me_x + x + n_x, n_x), me_c]

        def send_cot(z, x, send, recv, device):
            remote(cot_at(z, x), cot_at(z, x), send, recv.at[0], device).start()

        far_first(n_z, lambda k: send_cot(me_z, 0, cot_send, cot_recv, peer(k, 0)))

    with jax.named_scope("marks"):
        for i in (2, 3, 4, 5):
            loads[i].wait()
        lane = lax.broadcasted_iota(jnp.int32, (width, width), 1)
        sub = lax.broadcasted_iota(jnp.int32, (width, width), 0)
        tall = lax.broadcasted_iota(jnp.int32, (CORES * half, width), 0)
        one_lane = lax.broadcasted_iota(jnp.int32, (1, width), 1)
        last_window = cot.shape[0] - WINDOW // (CORES * rows)

        def hot(mask):
            return jnp.where(mask, 1.0, 0.0).astype(jnp.bfloat16)

        def mark(b):
            here = pl.ds(pl.multiple_of(b * width, width), width)
            ids = src[pl.ds(b, 1), :]
            picked = hot(jnp.broadcast_to(ids, (width, width)).T == lane)
            hot_src[here, 0:width] = picked
            hot_src[here, width : 2 * width] = picked
            owner = lax.rem((ids >> 4) + (n_src - me_s), n_src)
            hot_src_t[:, here] = hot(sub[: n_src * rows] == owner * rows + (ids & (rows - 1)))
            valid = one_lane < counts[b]
            start = offsets[b]
            target = rel[pl.ds(b, 1), :] + start
            owner = target >> 4
            core = lax.rem(owner + me_c, CORES)
            x = lax.rem((owner >> 1) + (n_x - me_x), n_x)
            z = lax.rem(lax.div(owner, CORES * n_x) + (n_z - me_z), n_z)
            place = ((core * n_x + x) * n_z + z) * rows + (target & (rows - 1))
            hot_dst[:, here] = hot(tall == jnp.where(valid, place, -1))
            base = jnp.minimum(start >> 5, last_window) * (CORES * rows)
            inside = jnp.broadcast_to(jnp.where(valid, target - base, -1), (width, width)).T
            hot_win[here, 0:width] = hot(inside == lane)
            hot_win[here, width : 2 * width] = hot(inside == lane + width)

        loop(0, blocks, mark)

    with jax.named_scope("attr_part"):
        for i in (6, 7, 8):
            loads[i].wait()
        tile = min(256, edges)

        def attr_part(i):
            here = pl.ds(pl.multiple_of(i * tile, tile), tile)
            pre[here, :] = (
                jnp.dot(attr[here, :], wedge[...], preferred_element_type=jnp.float32) + bias[...]
            )

        loop(0, edges // tile, attr_part, True)

    with jax.named_scope("feats_wait"):
        loads[9].wait()
        loads[10].wait()
        all_of(group.at[pl.ds(0, n_src - 1)], feat_send, feat_recv).wait_recv()

    with jax.named_scope("forward"):
        high, low = split_bf16(
            jnp.dot(
                group[...].reshape(n_src * rows, feat), wnode[...], preferred_element_type=jnp.float32
            )
        )
        if n_src * rows < width:
            proj[...] = jnp.zeros_like(proj)
        proj[0 : n_src * rows, :] = high
        proj[width : width + n_src * rows, :] = low

        def forward(i):
            here = pl.ds(pl.multiple_of(i * tile, tile), tile)
            value = pre[here, :] + jnp.dot(
                hot_src[here, :], proj[...], preferred_element_type=jnp.float32
            )
            sig = 0.5 * jnp.tanh(0.5 * value) + 0.5
            hidden = (value * sig).astype(jnp.bfloat16)
            pre[here, :] = sig * (1.0 + value * (1.0 - sig))
            msg[here, :] = jnp.dot(hidden, wout[...], preferred_element_type=jnp.float32).astype(
                jnp.bfloat16
            )

        loop(0, edges // tile, forward, True)

    with jax.named_scope("sums"):
        order = (across,) + tuple(k for k in range(1, n_x) if k != across) + (0,)

        def half_copy(k):
            part = pl.ds(k * slab, slab)
            return remote(half_out.at[part], half_in.at[part], half_send, half_recv.at[k], sibling)

        half_out[...] = jnp.dot(
            hot_dst[half : 2 * half, :], msg[...], preferred_element_type=jnp.float32
        ).astype(jnp.bfloat16)
        for k in order:
            half_copy(k).start()

    with jax.named_scope("cot_second"):
        all_of(cot.at[pl.ds(0, n_z - 1), 0], cot_send, cot_recv).wait_recv()

        def second(z):
            send_cot(z, 0, cz_send, cz_recv, peer(0, 1))
            send_cot(z, 0, cz_send, cz_recv, peer(0, -1))

        loop(0, n_z, second)
        loop(0, n_z, lambda z: send_cot(z, 0, cc_send, cc_recv, sibling))

    with jax.named_scope("sums_rest"):
        kept[...] = jnp.dot(hot_dst[0:half, :], msg[...], preferred_element_type=jnp.float32)
        slot = 0
        for k in order:
            part = slice(k * slab, (k + 1) * slab)
            half_copy(k).wait_recv()
            total = kept[part, :] + half_in[part, :].astype(jnp.float32)
            if k == across:
                far[...] = total[:rows]
                b_out[...] = total[rows:].astype(jnp.bfloat16).reshape(n_z - 1, rows, feat)
                far_first(
                    n_z,
                    lambda z: remote(
                        b_out.at[z - 1], b_in.at[z - 1], b_send, b_recv.at[0], peer(z, 0)
                    ).start(),
                )
            elif k:
                x_out[slot] = total.astype(jnp.bfloat16)
                remote(x_out.at[slot], x_in.at[slot], x_send, x_recv.at[0], peer(0, k)).start()
                slot += 1
            else:
                own[...] = total

    with jax.named_scope("cot_third"):
        all_of(cot.at[pl.ds(0, 2 * n_z), 0], cz_send, cz_recv).wait_recv()
        loop(0, n_z // 2, lambda z: send_cot(z, -1, relay_send, relay_recv, peer(0, 1)))
        loop(n_z // 2, n_z, lambda z: send_cot(z, 1, relay_send, relay_recv, peer(0, -1)))

        def pass_beside(z):
            send_cot(z, -1, cc_send, cc_recv, sibling)
            send_cot(z, 1, cc_send, cc_recv, sibling)

        loop(0, n_z, pass_beside)

    def backward(b):
        here = pl.ds(pl.multiple_of(b * width, width), width)
        first = jnp.minimum(offsets[b] >> 5, last_window)
        window = cot[pl.ds(first, WINDOW // (CORES * rows))].reshape(WINDOW, feat)
        d_message = jnp.dot(
            hot_win[here, :], window, preferred_element_type=jnp.float32
        ).astype(jnp.bfloat16)
        d_hidden = lax.dot_general(d_message, wout[...], NT, preferred_element_type=jnp.float32)
        d_pre = (d_hidden * pre[here, :]).astype(jnp.bfloat16)
        dpre[here, :] = d_pre
        attr_grad[here, :] = lax.dot_general(
            d_pre, wedge[...], NT, preferred_element_type=jnp.float32
        ).astype(jnp.bfloat16)

    with jax.named_scope("sums_x"):
        if n_x > 2:
            all_of(x_in, x_send, x_recv).wait_recv()
        summed = own[...]
        for k in range(n_x - 2):
            summed = summed + x_in[k].astype(jnp.float32)
        own[...] = summed
        z_out[...] = summed[rows:].astype(jnp.bfloat16).reshape(n_z - 1, rows, feat)
        far_first(
            n_z,
            lambda z: remote(
                z_out.at[z - 1], z_in.at[z - 1], z_send, z_recv.at[0], peer(z, 0)
            ).start(),
        )

    with jax.named_scope("cot_rest"):
        all_of(cot.at[pl.ds(0, n_z), 0], relay_send, relay_recv).wait_recv()
        loop(0, n_z, lambda z: send_cot(z, across, cc_send, cc_recv, sibling))

    with jax.named_scope("cot_last"):
        all_of(cot.at[:, 0], cc_send, cc_recv).wait_recv()

    with jax.named_scope("sums_far"):
        all_of(b_in, b_send, b_recv).wait_recv()
        far_out[...] = (far[...] + jnp.sum(b_in[...].astype(jnp.float32), axis=0)).astype(jnp.bfloat16)
        far_copy = remote(far_out, far_in, far_send, far_recv.at[0], peer(0, across))
        far_copy.start()

    with jax.named_scope("backward"):
        loop(0, blocks, backward, True)
        attr_store = pltpu.make_async_copy(attr_grad, attr_out, store_sem.at[0])
        attr_store.start()

    with jax.named_scope("source_sums"):
        high, low = split_bf16(
            jnp.dot(hot_src_t[...], dpre[...], preferred_element_type=jnp.float32)
        )
        sums = lax.dot_general(
            high, wnode[...], NT, preferred_element_type=jnp.float32
        ) + lax.dot_general(low, wnode[...], NT, preferred_element_type=jnp.float32)
        node_own = sums[:rows]
        s_out[...] = sums[rows:].astype(jnp.bfloat16).reshape(n_src - 1, rows, feat)
        far_first(
            n_src,
            lambda k: remote(
                s_out.at[k - 1], s_in.at[k - 1], s_send, s_recv.at[0], y_peer(k)
            ).start(),
        )

    with jax.named_scope("drain"):
        all_of(group.at[pl.ds(0, n_src - 1)], feat_send, feat_recv).wait_send()
        all_of(cot.at[pl.ds(0, n_z - 1), 0], cot_send, cot_recv).wait_send()
        all_of(cot.at[pl.ds(0, 2 * n_z), 0], cz_send, cz_recv).wait_send()
        all_of(cot.at[pl.ds(0, n_z), 0], relay_send, relay_recv).wait_send()
        all_of(cot.at[:, 0], cc_send, cc_recv).wait_send()
        all_of(half_out, half_send, half_recv).wait_send()
        if n_x > 2:
            all_of(x_out, x_send, x_recv).wait_send()
        all_of(b_out, b_send, b_recv).wait_send()
        attr_store.wait()

    with jax.named_scope("last_z"):
        all_of(z_in, z_send, z_recv).wait_recv()
        partial = own[0:rows, :] + jnp.sum(z_in[...].astype(jnp.float32), axis=0)

    with jax.named_scope("last_far"):
        far_copy.wait_recv()
        agg[...] = (partial + far_in[...].astype(jnp.float32)).astype(jnp.bfloat16)
        agg_store = pltpu.make_async_copy(agg, agg_out, store_sem.at[1])
        agg_store.start()

    with jax.named_scope("last_y"):
        all_of(s_in, s_send, s_recv).wait_recv()
        node[...] = (node_own + jnp.sum(s_in[...].astype(jnp.float32), axis=0)).astype(jnp.bfloat16)
        node_store = pltpu.make_async_copy(node, node_out, store_sem.at[2])
        node_store.start()

    with jax.named_scope("drain_last"):
        all_of(z_out, z_send, z_recv).wait_send()
        far_copy.wait_send()
        all_of(s_out, s_send, s_recv).wait_send()
        agg_store.wait()
        node_store.wait()


def write(*refs):
    count = len(refs) // 2
    sem = refs[-1]
    copies = [
        pltpu.make_async_copy(refs[i], refs[count + i], sem.at[i]) for i in range(count)
    ]
    for copy in copies:
        copy.start()
    for copy in copies:
        copy.wait()


def local(
    n_src, n_x, n_z,
    node_feats, cotangent, edge_attr, src_ids, dst_rel, offsets, counts, w_node, w_edge, bias, w_out,
):
    rows, feat = node_feats.shape
    edges, attr_width = edge_attr.shape
    blocks = offsets.shape[0]
    width = edges // blocks
    hidden = w_node.shape[1]
    slab = rows * n_z
    half = slab * n_x
    f32, bf16 = jnp.float32, jnp.bfloat16
    vmem, dma = pltpu.VMEM, pltpu.SemaphoreType.DMA
    anywhere = pl.BlockSpec(memory_space=pl.ANY)
    operands = (
        node_feats, cotangent, edge_attr,
        src_ids.reshape(blocks, width), dst_rel.reshape(blocks, width), offsets, counts,
        w_node, w_edge, bias.reshape(1, hidden), w_out,
    )
    outs = (
        jax.ShapeDtypeStruct((rows, feat), bf16),
        jax.ShapeDtypeStruct((rows, feat), bf16),
        jax.ShapeDtypeStruct((edges, attr_width), bf16),
    )
    results = pl.pallas_call(
        functools.partial(kernel, (n_src, n_x, n_z, rows)),
        out_shape=outs,
        in_specs=[anywhere] * len(operands),
        out_specs=(anywhere,) * 3,
        scratch_shapes=[
            pltpu.SMEM((blocks,), jnp.int32),
            pltpu.SMEM((blocks,), jnp.int32),
            vmem((n_src, rows, feat), bf16),
            vmem((n_z * n_x, CORES, rows, feat), bf16),
            vmem((edges, attr_width), bf16),
            vmem((blocks, width), jnp.int32),
            vmem((blocks, width), jnp.int32),
            vmem(w_node.shape, bf16),
            vmem(w_edge.shape, bf16),
            vmem((1, hidden), f32),
            vmem(w_out.shape, bf16),
            vmem((edges, 2 * width), bf16),
            vmem((n_src * rows, edges), bf16),
            vmem((CORES * half, edges), bf16),
            vmem((edges, WINDOW), bf16),
            vmem((2 * width, hidden), bf16),
            vmem((edges, hidden), f32),
            vmem((edges, feat), bf16),
            vmem((edges, hidden), bf16),
            vmem((edges, attr_width), bf16),
            vmem((half, feat), bf16),
            vmem((half, feat), bf16),
            vmem((half, feat), f32),
            vmem((slab, feat), f32),
            vmem((rows, feat), f32),
            vmem((max(n_x - 2, 1), slab, feat), bf16),
            vmem((max(n_x - 2, 1), slab, feat), bf16),
            vmem((n_z - 1, rows, feat), bf16),
            vmem((n_z - 1, rows, feat), bf16),
            vmem((rows, feat), bf16),
            vmem((rows, feat), bf16),
            vmem((n_z - 1, rows, feat), bf16),
            vmem((n_z - 1, rows, feat), bf16),
            vmem((n_src - 1, rows, feat), bf16),
            vmem((n_src - 1, rows, feat), bf16),
            vmem((rows, feat), bf16),
            vmem((rows, feat), bf16),
            dma((len(operands),)),
            dma((n_x,)),
            dma((3,)),
        ]
        + [dma((1,))] * 21,
        compiler_params=pltpu.CompilerParams(
            collective_id=0, has_side_effects=True, vmem_limit_bytes=32 * 1024 * 1024
        ),
    )(*(pltpu.with_memory_space_constraint(operand, pltpu.HBM) for operand in operands))
    return pl.pallas_call(
        write,
        out_shape=outs,
        in_specs=[anywhere] * 3,
        out_specs=(anywhere,) * 3,
        scratch_shapes=[dma((3,))],
    )(*(pltpu.with_memory_space_constraint(result, pltpu.VMEM) for result in results))


def build(mesh, n_x):
    n_src, n_dst = mesh.shape["src"], mesh.shape["dst"]
    in_specs = (
        P(("dst", "src"), None),
        P(("src", "dst"), None),
        P(("src", "dst"), None),
        P(("src", "dst")),
        P(("src", "dst")),
        P(("src", "dst")),
        P(("src", "dst")),
        P(),
        P(),
        P(),
        P(),
    )
    out_specs = (P(("src", "dst"), None), P(("dst", "src"), None), P(("src", "dst"), None))
    return jax.shard_map(
        functools.partial(local, n_src, n_x, n_dst // (n_x * CORES)),
        mesh=mesh, in_specs=in_specs, out_specs=out_specs, check_vma=False,
    )


def solution(mesh):
    return build(mesh, X_CHIPS)
```

```python
import functools

import jax
import jax.numpy as jnp
from jax import lax
from jax.experimental import pallas as pl
from jax.experimental.pallas import tpu as pltpu
from jax.sharding import PartitionSpec as P

MESH = pl.DeviceIdType.MESH
X_CHIPS = 4
CORES = 2
WINDOW = 256
NT = (((1,), (1,)), ((), ()))


def split_bf16(value):
    high = value.astype(jnp.bfloat16)
    low = (value - high.astype(jnp.float32)).astype(jnp.bfloat16)
    return high, low


def loop(first, last, step, unroll=1):
    def body(k, carry):
        step(k)
        return carry

    lax.fori_loop(first, last, body, 0, unroll=unroll)


def far_first(size, step, first=0, last=None):
    def body(i):
        step(size // 2 + (1 - 2 * lax.rem(i, 2)) * lax.div(i + 1, 2))

    loop(first, size - 1 if last is None else last, body)


def kernel(
    dims,
    feats_in, cot_in, attr_in, src_in, rel_in, offsets_in, counts_in, wnode_in, wedge_in, bias_in,
    wout_in,
    agg_out, node_out, attr_out,
    offsets, counts, group, cot, attr, src, rel, wnode, wedge, bias, wout,
    hot_src, hot_src_t, hot_dst, hot_win,
    proj, pre, msg, hidden, attr_grad,
    half_out, half_in, kept, own, far, x_out, x_in, b_out, b_in, far_out, far_in, z_out, z_in, s_out, s_in,
    agg, node,
    load_sem, half_recv, store_sem, cot_recv, cz_recv,
    feat_send, feat_recv, cot_send, cz_send, relay_send, relay_recv, cc_send, cc_recv, half_send,
    x_send, x_recv, b_send, b_recv, far_send, far_recv, z_send, z_recv, s_send, s_recv,
):
    n_src, n_x, n_z, rows = dims
    blocks, width = src.shape
    edges = blocks * width
    feat = group.shape[2]
    me_s = lax.axis_index("src")
    me_d = lax.axis_index("dst")
    me_c = lax.rem(me_d, CORES)
    me_x = lax.rem(lax.div(me_d, CORES), n_x)
    me_z = lax.div(me_d, CORES * n_x)
    slab = rows * n_z
    half = slab * n_x
    across = n_x // 2
    reach = n_z // 4
    near = 2 * reach + 1

    def dst_at(z, x, c):
        return (z * n_x + x) * CORES + c

    def y_peer(k):
        return (lax.rem(me_s + k, n_src), me_d)

    def peer(z, x):
        return (
            me_s, dst_at(lax.rem(me_z + z + n_z, n_z), lax.rem(me_x + x + n_x, n_x), me_c),
        )

    sibling = (me_s, dst_at(me_z, me_x, 1 - me_c))

    def remote(source, target, send, recv, device):
        return pltpu.make_async_remote_copy(
            src_ref=source, dst_ref=target, send_sem=send.at[0], recv_sem=recv,
            device_id=device, device_id_type=MESH,
        )

    def all_of(ref, send, recv):
        return remote(ref, ref, send, recv.at[0], sibling)


    with jax.named_scope("load"):
        loads = [
            pltpu.make_async_copy(source, target, load_sem.at[i])
            for i, (source, target) in enumerate(
                (
                    (feats_in, group.at[me_s]), (cot_in, cot.at[me_z * n_x + me_x, me_c]),
                    (src_in, src), (rel_in, rel), (offsets_in, offsets), (counts_in, counts),
                    (attr_in, attr), (wedge_in, wedge), (bias_in, bias),
                    (wnode_in, wnode), (wout_in, wout),
                )
            )
        ]
        for load in loads:
            load.start()

    with jax.named_scope("barrier"):
        barrier = pltpu.get_barrier_semaphore()

        def greet(device):
            pl.semaphore_signal(barrier, inc=1, device_id=device, device_id_type=MESH)

        far_first(n_src, lambda k: greet(y_peer(k)))
        far_first(n_z, lambda k: greet(peer(k, 0)))
        for k in range(1, n_x):
            greet(peer(0, k))
        greet(sibling)
        loads[0].wait()
        loads[1].wait()
        pl.semaphore_wait(barrier, (n_src - 1) + (n_z - 1) + (n_x - 1) + 1)

    with jax.named_scope("first_sends"):
        mine = group.at[me_s]
        far_first(
            n_src, lambda k: remote(mine, mine, feat_send, feat_recv.at[0], y_peer(k)).start()
        )

        def cot_at(j, x):
            z = lax.rem(me_z + (n_z - reach) + j, n_z)
            return cot.at[z * n_x + lax.rem(me_x + x + n_x, n_x), me_c]

        def send_cot(j, x, send, recv, device):
            remote(cot_at(j, x), cot_at(j, x), send, recv, device).start()

        def cot_bytes(count, send, recv):
            return remote(cot.at[pl.ds(0, count), 0], cot.at[pl.ds(0, count), 0], send, recv, sibling)

        def to_sibling(j, x):
            send_cot(j, x, cc_send, cc_recv.at[0], sibling)

        for k in range(reach, 0, -1):
            send_cot(reach, 0, cot_send, cot_recv.at[0], peer(k, 0))
            send_cot(reach, 0, cot_send, cot_recv.at[0], peer(-k, 0))
        loop(
            reach + 1,
            n_z - reach,
            lambda k: send_cot(reach, 0, cot_send, cot_recv.at[1], peer(k, 0)),
        )

        def second(j):
            send_cot(j, 0, cz_send, cz_recv.at[0], peer(0, 1))
            send_cot(j, 0, cz_send, cz_recv.at[0], peer(0, -1))

        def second_far(j):
            for k in (across, 1, -1):
                send_cot(j, 0, cz_send, cz_recv.at[1], peer(0, k))

        def pass_beside(j):
            to_sibling(j, -1)
            to_sibling(j, 1)

    with jax.named_scope("marks"):
        for i in (2, 3, 4, 5):
            loads[i].wait()
        lane = lax.broadcasted_iota(jnp.int32, (width, width), 1)
        sub = lax.broadcasted_iota(jnp.int32, (width, width), 0)
        tall = lax.broadcasted_iota(jnp.int32, (CORES * half, width), 0)
        one_lane = lax.broadcasted_iota(jnp.int32, (1, width), 1)
        last_window = cot.shape[0] - WINDOW // (CORES * rows)

        def hot(mask):
            return jnp.where(mask, 1.0, 0.0).astype(jnp.bfloat16)

        def mark(b):
            here = pl.ds(pl.multiple_of(b * width, width), width)
            ids = src[pl.ds(b, 1), :]
            picked = hot(jnp.broadcast_to(ids, (width, width)).T == lane)
            hot_src[here, 0:width] = picked
            hot_src[here, width : 2 * width] = picked
            owner = lax.rem((ids >> 4) + (n_src - me_s), n_src)
            hot_src_t[:, here] = hot(sub[: n_src * rows] == owner * rows + (ids & (rows - 1)))
            valid = one_lane < counts[b]
            start = offsets[b]
            target = rel[pl.ds(b, 1), :] + start
            owner = target >> 4
            core = lax.rem(owner + me_c, CORES)
            x = lax.rem((owner >> 1) + (n_x - me_x), n_x)
            z = lax.rem(lax.div(owner, CORES * n_x) + (n_z - me_z), n_z)
            place = ((core * n_x + x) * n_z + z) * rows + (target & (rows - 1))
            hot_dst[:, here] = hot(tall == jnp.where(valid, place, -1))
            base = jnp.minimum(start >> 5, last_window) * (CORES * rows)
            inside = jnp.broadcast_to(jnp.where(valid, target - base, -1), (width, width)).T
            hot_win[here, 0:width] = 0.5 * hot(inside == lane)
            hot_win[here, width : 2 * width] = 0.5 * hot(inside == lane + width)

        loop(0, blocks, mark)

    with jax.named_scope("attr_part"):
        for i in (6, 7, 8):
            loads[i].wait()
        tile = min(256, edges)

        def attr_part(i):
            here = pl.ds(pl.multiple_of(i * tile, tile), tile)
            pre[here, :] = 0.5 * (
                jnp.dot(attr[here, :], wedge[...], preferred_element_type=jnp.float32) + bias[...]
            )

        loop(0, edges // tile, attr_part, True)

    with jax.named_scope("feats_wait"):
        loads[9].wait()
        loads[10].wait()
        all_of(group.at[pl.ds(0, n_src - 1)], feat_send, feat_recv).wait_recv()

    with jax.named_scope("forward"):
        high, low = split_bf16(
            0.5
            * jnp.dot(
                group[...].reshape(n_src * rows, feat), wnode[...], preferred_element_type=jnp.float32
            )
        )
        if n_src * rows < width:
            proj[...] = jnp.zeros_like(proj)
        proj[0 : n_src * rows, :] = high
        proj[width : width + n_src * rows, :] = low

        def activate(i):
            here = slice(i * tile, (i + 1) * tile)
            value = pre[here, :] + jnp.dot(
                hot_src[here, :], proj[...], preferred_element_type=jnp.float32
            )
            rise = 1.0 + jnp.tanh(value)
            silu = value * rise
            hidden[here, :] = silu.astype(jnp.bfloat16)
            pre[here, :] = rise + silu * (2.0 - rise)

        def project(i):
            here = slice(i * tile, (i + 1) * tile)
            msg[here, :] = jnp.dot(
                hidden[here, :], wout[...], preferred_element_type=jnp.float32
            ).astype(jnp.bfloat16)

        tiles = edges // tile
        early = tiles // 3
        for i in range(early):
            activate(i)

    with jax.named_scope("cot_near"):
        cot_bytes(near - 1, cot_send, cot_recv.at[0]).wait_recv()
        loop(0, near, second)
        loop(0, near, lambda j: to_sibling(j, 0))

    with jax.named_scope("forward_rest"):
        for i in range(early, tiles):
            activate(i)
            project(i - early)
        for i in range(tiles - early, tiles):
            project(i)

    with jax.named_scope("sums"):
        order = (across,) + tuple(k for k in range(1, n_x) if k != across) + (0,)

        def half_copy(k):
            part = pl.ds(k * slab, slab)
            return remote(half_out.at[part], half_in.at[part], half_send, half_recv.at[k], sibling)

        piece = half // 2

        def gather_half(i):
            here = pl.ds(pl.multiple_of(i * piece, piece), piece)
            there = pl.ds(pl.multiple_of(half + i * piece, piece), piece)
            half_out[here, :] = jnp.dot(
                hot_dst[there, :], msg[...], preferred_element_type=jnp.float32
            ).astype(jnp.bfloat16)

        loop(0, 2, gather_half)
        for k in order:
            half_copy(k).start()

    with jax.named_scope("cot_far"):
        cot_bytes(n_z - near, cot_send, cot_recv.at[1]).wait_recv()
        loop(near, n_z, second_far)

    with jax.named_scope("sums_rest"):
        def gather_kept(i):
            here = pl.ds(pl.multiple_of(i * piece, piece), piece)
            kept[here, :] = jnp.dot(hot_dst[here, :], msg[...], preferred_element_type=jnp.float32)

        loop(0, 2, gather_kept)

    with jax.named_scope("cot_third"):
        cot_bytes(2 * near, cz_send, cz_recv.at[0]).wait_recv()
        loop(0, near // 2, lambda j: send_cot(j, -1, relay_send, relay_recv.at[0], peer(0, 1)))
        loop(near // 2, near, lambda j: send_cot(j, 1, relay_send, relay_recv.at[0], peer(0, -1)))

    with jax.named_scope("sums_both"):
        slot = 0
        for k in order:
            part = slice(k * slab, (k + 1) * slab)
            half_copy(k).wait_recv()
            total = kept[part, :] + half_in[part, :].astype(jnp.float32)
            if k == across:
                far[...] = total[:rows]
                b_out[...] = total[rows:].astype(jnp.bfloat16).reshape(n_z - 1, rows, feat)
                far_first(
                    n_z,
                    lambda z: remote(
                        b_out.at[z - 1], b_in.at[z - 1], b_send, b_recv.at[0], peer(z, 0)
                    ).start(),
                )
            elif k:
                x_out[slot] = total.astype(jnp.bfloat16)
                remote(x_out.at[slot], x_in.at[slot], x_send, x_recv.at[0], peer(0, k)).start()
                slot += 1
            else:
                own[...] = total

    with jax.named_scope("cot_rest"):
        loop(near, n_z, lambda j: to_sibling(j, 0))
        loop(0, near, pass_beside)
        cot_bytes(near, relay_send, relay_recv.at[0]).wait_recv()
        loop(0, near, lambda j: to_sibling(j, across))

    with jax.named_scope("cot_rest_far"):
        cot_bytes((n_x - 1) * (n_z - near), cz_send, cz_recv.at[1]).wait_recv()

        def pass_far(j):
            for k in (across, 1, -1):
                to_sibling(j, k)

        loop(near, n_z, pass_far)

    with jax.named_scope("sums_x"):
        if n_x > 2:
            all_of(x_in, x_send, x_recv).wait_recv()
        summed = own[...]
        for k in range(n_x - 2):
            summed = summed + x_in[k].astype(jnp.float32)
        own[...] = summed
        z_out[...] = summed[rows:].astype(jnp.bfloat16).reshape(n_z - 1, rows, feat)
        far_first(
            n_z,
            lambda z: remote(
                z_out.at[z - 1], z_in.at[z - 1], z_send, z_recv.at[0], peer(z, 0)
            ).start(),
        )

    with jax.named_scope("cot_last"):
        all_of(cot.at[:, 0], cc_send, cc_recv).wait_recv()

    with jax.named_scope("backward"):
        for i in range(blocks):
            here = slice(i * width, (i + 1) * width)
            first = jnp.minimum(offsets[i] >> 5, last_window)
            window = cot[pl.ds(first, WINDOW // (CORES * rows))].reshape(WINDOW, feat)
            msg[here, :] = jnp.dot(
                hot_win[here, :], window, preferred_element_type=jnp.float32
            ).astype(jnp.bfloat16)

    with jax.named_scope("d_pre"):
        wide = min(512, edges)
        for i in range(edges // wide):
            here = slice(i * wide, (i + 1) * wide)
            d_hidden = lax.dot_general(
                msg[here, :], wout[...], NT, preferred_element_type=jnp.float32
            )
            hidden[here, :] = (d_hidden * pre[here, :]).astype(jnp.bfloat16)

    with jax.named_scope("source_sums"):
        high, low = split_bf16(
            jnp.dot(hot_src_t[...], hidden[...], preferred_element_type=jnp.float32)
        )
        sums = lax.dot_general(
            high, wnode[...], NT, preferred_element_type=jnp.float32
        ) + lax.dot_general(low, wnode[...], NT, preferred_element_type=jnp.float32)
        node_own = sums[:rows]
        s_out[...] = sums[rows:].astype(jnp.bfloat16).reshape(n_src - 1, rows, feat)
        far_first(
            n_src,
            lambda k: remote(
                s_out.at[k - 1], s_in.at[k - 1], s_send, s_recv.at[0], y_peer(k)
            ).start(),
        )

    with jax.named_scope("sums_far"):
        all_of(b_in, b_send, b_recv).wait_recv()
        far_out[...] = (far[...] + jnp.sum(b_in[...].astype(jnp.float32), axis=0)).astype(jnp.bfloat16)
        far_copy = remote(far_out, far_in, far_send, far_recv.at[0], peer(0, across))
        far_copy.start()

    with jax.named_scope("attr_grads"):
        for i in range(edges // wide):
            here = slice(i * wide, (i + 1) * wide)
            attr_grad[here, :] = lax.dot_general(
                hidden[here, :], wedge[...], NT, preferred_element_type=jnp.float32
            ).astype(jnp.bfloat16)
        attr_store = pltpu.make_async_copy(attr_grad, attr_out, store_sem.at[0])
        attr_store.start()

    with jax.named_scope("drain"):
        all_of(group.at[pl.ds(0, n_src - 1)], feat_send, feat_recv).wait_send()
        cot_bytes(n_z - 1, cot_send, cot_recv.at[0]).wait_send()
        cot_bytes(2 * near + (n_x - 1) * (n_z - near), cz_send, cz_recv.at[0]).wait_send()
        cot_bytes(near, relay_send, relay_recv.at[0]).wait_send()
        all_of(cot.at[:, 0], cc_send, cc_recv).wait_send()
        all_of(half_out, half_send, half_recv).wait_send()
        if n_x > 2:
            all_of(x_out, x_send, x_recv).wait_send()
        all_of(b_out, b_send, b_recv).wait_send()

    with jax.named_scope("last_z"):
        all_of(z_in, z_send, z_recv).wait_recv()
        partial = own[0:rows, :] + jnp.sum(z_in[...].astype(jnp.float32), axis=0)

    with jax.named_scope("last_far"):
        far_copy.wait_recv()
        agg[...] = (partial + far_in[...].astype(jnp.float32)).astype(jnp.bfloat16)
        agg_store = pltpu.make_async_copy(agg, agg_out, store_sem.at[1])
        agg_store.start()

    with jax.named_scope("last_y"):
        all_of(s_in, s_send, s_recv).wait_recv()
        node[...] = (node_own + jnp.sum(s_in[...].astype(jnp.float32), axis=0)).astype(jnp.bfloat16)
        node_store = pltpu.make_async_copy(node, node_out, store_sem.at[2])
        node_store.start()

    with jax.named_scope("drain_last"):
        all_of(z_out, z_send, z_recv).wait_send()
        far_copy.wait_send()
        all_of(s_out, s_send, s_recv).wait_send()
        attr_store.wait()
        agg_store.wait()
        node_store.wait()


def write(*refs):
    count = len(refs) // 2
    sem = refs[-1]
    copies = [
        pltpu.make_async_copy(refs[i], refs[count + i], sem.at[i]) for i in range(count)
    ]
    for copy in copies:
        copy.start()
    for copy in copies:
        copy.wait()


def local(
    n_src, n_x, n_z,
    node_feats, cotangent, edge_attr, src_ids, dst_rel, offsets, counts, w_node, w_edge, bias, w_out,
):
    rows, feat = node_feats.shape
    edges, attr_width = edge_attr.shape
    blocks = offsets.shape[0]
    width = edges // blocks
    hidden = w_node.shape[1]
    slab = rows * n_z
    half = slab * n_x
    f32, bf16 = jnp.float32, jnp.bfloat16
    vmem, dma = pltpu.VMEM, pltpu.SemaphoreType.DMA
    anywhere = pl.BlockSpec(memory_space=pl.ANY)
    operands = (
        node_feats, cotangent, edge_attr,
        src_ids.reshape(blocks, width), dst_rel.reshape(blocks, width), offsets, counts,
        w_node, w_edge, bias.reshape(1, hidden), w_out,
    )
    outs = (
        jax.ShapeDtypeStruct((rows, feat), bf16),
        jax.ShapeDtypeStruct((rows, feat), bf16),
        jax.ShapeDtypeStruct((edges, attr_width), bf16),
    )
    results = pl.pallas_call(
        functools.partial(kernel, (n_src, n_x, n_z, rows)),
        out_shape=outs,
        in_specs=[anywhere] * len(operands),
        out_specs=(anywhere,) * 3,
        scratch_shapes=[
            pltpu.SMEM((blocks,), jnp.int32),
            pltpu.SMEM((blocks,), jnp.int32),
            vmem((n_src, rows, feat), bf16),
            vmem((n_z * n_x, CORES, rows, feat), bf16),
            vmem((edges, attr_width), bf16),
            vmem((blocks, width), jnp.int32),
            vmem((blocks, width), jnp.int32),
            vmem(w_node.shape, bf16),
            vmem(w_edge.shape, bf16),
            vmem((1, hidden), f32),
            vmem(w_out.shape, bf16),
            vmem((edges, 2 * width), bf16),
            vmem((n_src * rows, edges), bf16),
            vmem((CORES * half, edges), bf16),
            vmem((edges, WINDOW), bf16),
            vmem((2 * width, hidden), bf16),
            vmem((edges, hidden), f32),
            vmem((edges, feat), bf16),
            vmem((edges, hidden), bf16),
            vmem((edges, attr_width), bf16),
            vmem((half, feat), bf16),
            vmem((half, feat), bf16),
            vmem((half, feat), f32),
            vmem((slab, feat), f32),
            vmem((rows, feat), f32),
            vmem((max(n_x - 2, 1), slab, feat), bf16),
            vmem((max(n_x - 2, 1), slab, feat), bf16),
            vmem((n_z - 1, rows, feat), bf16),
            vmem((n_z - 1, rows, feat), bf16),
            vmem((rows, feat), bf16),
            vmem((rows, feat), bf16),
            vmem((n_z - 1, rows, feat), bf16),
            vmem((n_z - 1, rows, feat), bf16),
            vmem((n_src - 1, rows, feat), bf16),
            vmem((n_src - 1, rows, feat), bf16),
            vmem((rows, feat), bf16),
            vmem((rows, feat), bf16),
            dma((len(operands),)),
            dma((n_x,)),
            dma((3,)),
            dma((2,)),
            dma((2,)),
        ]
        + [dma((1,))] * 19,
        compiler_params=pltpu.CompilerParams(
            collective_id=0, has_side_effects=True, vmem_limit_bytes=32 * 1024 * 1024
        ),
    )(*(pltpu.with_memory_space_constraint(operand, pltpu.HBM) for operand in operands))
    return pl.pallas_call(
        write,
        out_shape=outs,
        in_specs=[anywhere] * 3,
        out_specs=(anywhere,) * 3,
        scratch_shapes=[dma((3,))],
    )(*(pltpu.with_memory_space_constraint(result, pltpu.VMEM) for result in results))


def build(mesh, n_x):
    n_src, n_dst = mesh.shape["src"], mesh.shape["dst"]
    in_specs = (
        P(("dst", "src"), None),
        P(("src", "dst"), None),
        P(("src", "dst"), None),
        P(("src", "dst")),
        P(("src", "dst")),
        P(("src", "dst")),
        P(("src", "dst")),
        P(),
        P(),
        P(),
        P(),
    )
    out_specs = (P(("src", "dst"), None), P(("dst", "src"), None), P(("src", "dst"), None))
    return jax.shard_map(
        functools.partial(local, n_src, n_x, n_dst // (n_x * CORES)),
        mesh=mesh, in_specs=in_specs, out_specs=out_specs, check_vma=False,
    )


def solution(mesh):
    return build(mesh, X_CHIPS)
```

```python
import functools

import jax
import jax.numpy as jnp
from jax import lax
from jax.experimental import pallas as pl
from jax.experimental.pallas import tpu as pltpu
from jax.sharding import PartitionSpec as P

MESH = pl.DeviceIdType.MESH
X_CHIPS = 4
CORES = 2
WINDOW = 256
NT = (((1,), (1,)), ((), ()))


def split_bf16(value):
    high = value.astype(jnp.bfloat16)
    low = (value - high.astype(jnp.float32)).astype(jnp.bfloat16)
    return high, low


def loop(first, last, step, unroll=1):
    def body(k, carry):
        step(k)
        return carry

    lax.fori_loop(first, last, body, 0, unroll=unroll)


def far_first(size, step, first=0, last=None):
    def body(i):
        step(size // 2 + (1 - 2 * lax.rem(i, 2)) * lax.div(i + 1, 2))

    loop(first, size - 1 if last is None else last, body)


def kernel(
    dims,
    feats_in, cot_in, attr_in, src_in, rel_in, offsets_in, counts_in, wnode_in, wedge_in, bias_in,
    wout_in,
    agg_out, node_out, attr_out,
    offsets, counts, group, cot, attr, src, rel, wnode, wedge, bias, wout,
    hot_src, hot_src_t, hot_dst, hot_win,
    proj, pre, msg, hidden, attr_grad,
    half_out, half_in, kept, own, far, x_out, x_in, b_out, b_in, far_out, far_in, z_out, z_in, s_out, s_in,
    agg, node,
    load_sem, half_recv, store_sem, cot_recv, cz_recv,
    feat_send, feat_recv, cot_send, cz_send, relay_send, relay_recv, cc_send, cc_recv, half_send,
    x_send, x_recv, b_send, b_recv, far_send, far_recv, z_send, z_recv, s_send, s_recv,
):
    n_src, n_x, n_z, rows = dims
    blocks, width = src.shape
    edges = blocks * width
    feat = group.shape[2]
    me_s = lax.axis_index("src")
    me_d = lax.axis_index("dst")
    me_c = lax.rem(me_d, CORES)
    me_x = lax.rem(lax.div(me_d, CORES), n_x)
    me_z = lax.div(me_d, CORES * n_x)
    slab = rows * n_z
    half = slab * n_x
    across = n_x // 2
    reach = n_z // 4
    near = 2 * reach + 1

    def dst_at(z, x, c):
        return (z * n_x + x) * CORES + c

    def y_peer(k):
        return (lax.rem(me_s + k + n_src, n_src), me_d)

    def peer(z, x):
        return (
            me_s, dst_at(lax.rem(me_z + z + n_z, n_z), lax.rem(me_x + x + n_x, n_x), me_c),
        )

    sibling = (me_s, dst_at(me_z, me_x, 1 - me_c))

    def remote(source, target, send, recv, device):
        return pltpu.make_async_remote_copy(
            src_ref=source, dst_ref=target, send_sem=send.at[0], recv_sem=recv,
            device_id=device, device_id_type=MESH,
        )

    def all_of(ref, send, recv):
        return remote(ref, ref, send, recv.at[0], sibling)


    with jax.named_scope("load"):
        loads = [
            pltpu.make_async_copy(source, target, load_sem.at[i])
            for i, (source, target) in enumerate(
                (
                    (src_in, src), (rel_in, rel), (offsets_in, offsets), (counts_in, counts),
                    (feats_in, group.at[me_s]), (cot_in, cot.at[me_z * n_x + me_x, me_c]),
                    (attr_in, attr), (wedge_in, wedge), (bias_in, bias),
                    (wnode_in, wnode), (wout_in, wout),
                )
            )
        ]
        for load in loads:
            load.start()

    with jax.named_scope("greet"):
        barrier = pltpu.get_barrier_semaphore()

        def greet(device):
            pl.semaphore_signal(barrier, inc=1, device_id=device, device_id_type=MESH)

        far_first(n_src, lambda k: greet(y_peer(k)))
        for k in range(reach, 0, -1):
            greet(peer(k, 0))
            greet(peer(-k, 0))
        for k in range(1, n_x):
            greet(peer(0, k))
        greet(sibling)

    with jax.named_scope("marks_first"):
        for i in range(4):
            loads[i].wait()
        lane = lax.broadcasted_iota(jnp.int32, (width, width), 1)
        sub = lax.broadcasted_iota(jnp.int32, (width, width), 0)
        tall = lax.broadcasted_iota(jnp.int32, (CORES * half, width), 0)
        one_lane = lax.broadcasted_iota(jnp.int32, (1, width), 1)
        last_window = cot.shape[0] - WINDOW // (CORES * rows)

        def hot(mask):
            return jnp.where(mask, 1.0, 0.0).astype(jnp.bfloat16)

        def mark(b):
            here = pl.ds(pl.multiple_of(b * width, width), width)
            ids = src[pl.ds(b, 1), :]
            picked = hot(jnp.broadcast_to(ids, (width, width)).T == lane)
            hot_src[here, 0:width] = picked
            hot_src[here, width : 2 * width] = picked
            owner = lax.rem((ids >> 4) + (n_src - me_s), n_src)
            hot_src_t[:, here] = hot(sub[: n_src * rows] == owner * rows + (ids & (rows - 1)))
            valid = one_lane < counts[b]
            start = offsets[b]
            target = rel[pl.ds(b, 1), :] + start
            owner = target >> 4
            core = lax.rem(owner + me_c, CORES)
            x = lax.rem((owner >> 1) + (n_x - me_x), n_x)
            z = lax.rem(lax.div(owner, CORES * n_x) + (n_z - me_z), n_z)
            place = ((core * n_x + x) * n_z + z) * rows + (target & (rows - 1))
            hot_dst[:, here] = hot(tall == jnp.where(valid, place, -1))
            base = jnp.minimum(start >> 5, last_window) * (CORES * rows)
            inside = jnp.broadcast_to(jnp.where(valid, target - base, -1), (width, width)).T
            hot_win[here, 0:width] = 0.5 * hot(inside == lane)
            hot_win[here, width : 2 * width] = 0.5 * hot(inside == lane + width)

        loop(0, blocks // 4, mark)

    with jax.named_scope("barrier"):
        loads[4].wait()
        loads[5].wait()
        pl.semaphore_wait(barrier, (n_src - 1) + 2 * reach + (n_x - 1) + 1)

    with jax.named_scope("first_sends"):
        def cot_at(j, x):
            z = lax.rem(me_z + (n_z - reach) + j, n_z)
            return cot.at[z * n_x + lax.rem(me_x + x + n_x, n_x), me_c]

        def send_cot(j, x, send, recv, device):
            remote(cot_at(j, x), cot_at(j, x), send, recv, device).start()

        def cot_bytes(count, send, recv):
            return remote(cot.at[pl.ds(0, count), 0], cot.at[pl.ds(0, count), 0], send, recv, sibling)

        def to_sibling(j, x):
            send_cot(j, x, cc_send, cc_recv.at[0], sibling)

        for k in range(reach, 0, -1):
            send_cot(reach, 0, cot_send, cot_recv.at[0], peer(k, 0))
            send_cot(reach, 0, cot_send, cot_recv.at[0], peer(-k, 0))
        mine = group.at[me_s]
        far_first(
            n_src, lambda k: remote(mine, mine, feat_send, feat_recv.at[0], y_peer(k)).start()
        )

        def second(j):
            send_cot(j, 0, cz_send, cz_recv.at[0], peer(0, 1))
            send_cot(j, 0, cz_send, cz_recv.at[0], peer(0, -1))

        def second_far(j):
            for k in (across, 1, -1):
                send_cot(j, 0, cz_send, cz_recv.at[1], peer(0, k))

        def pass_beside(j):
            to_sibling(j, -1)
            to_sibling(j, 1)

    with jax.named_scope("marks"):
        loop(blocks // 4, blocks, mark)

    with jax.named_scope("attr_part"):
        for i in (6, 7, 8):
            loads[i].wait()
        tile = min(256, edges)

        def attr_part(i):
            here = pl.ds(pl.multiple_of(i * tile, tile), tile)
            pre[here, :] = 0.5 * (
                jnp.dot(attr[here, :], wedge[...], preferred_element_type=jnp.float32) + bias[...]
            )

        loop(0, edges // tile, attr_part, True)

    with jax.named_scope("cot_near"):
        cot_bytes(near - 1, cot_send, cot_recv.at[0]).wait_recv()
        for o in range(reach, 0, -1):
            send_cot(reach + o, 0, cot_send, cot_recv.at[1], peer(-reach, 0))
        for o in range(n_z - 3 * reach - 1, 0, -1):
            send_cot(reach - o, 0, cot_send, cot_recv.at[1], peer(reach, 0))
        loop(0, near, second)
        loop(0, near, lambda j: to_sibling(j, 0))

    with jax.named_scope("feats_wait"):
        loads[9].wait()
        loads[10].wait()
        all_of(group.at[pl.ds(0, n_src - 1)], feat_send, feat_recv).wait_recv()

    with jax.named_scope("forward"):
        high, low = split_bf16(
            0.5
            * jnp.dot(
                group[...].reshape(n_src * rows, feat), wnode[...], preferred_element_type=jnp.float32
            )
        )
        if n_src * rows < width:
            proj[...] = jnp.zeros_like(proj)
        proj[0 : n_src * rows, :] = high
        proj[width : width + n_src * rows, :] = low

        def activate(i):
            here = slice(i * tile, (i + 1) * tile)
            value = pre[here, :] + jnp.dot(
                hot_src[here, :], proj[...], preferred_element_type=jnp.float32
            )
            rise = 1.0 + jnp.tanh(value)
            silu = value * rise
            hidden[here, :] = silu.astype(jnp.bfloat16)
            pre[here, :] = rise + silu * (2.0 - rise)

        def project(i):
            here = slice(i * tile, (i + 1) * tile)
            msg[here, :] = jnp.dot(
                hidden[here, :], wout[...], preferred_element_type=jnp.float32
            ).astype(jnp.bfloat16)

        tiles = edges // tile
        activate(0)
        for i in range(1, tiles):
            activate(i)
            project(i - 1)
        project(tiles - 1)

    with jax.named_scope("sums"):
        piece = half // 2

        def half_copy(j):
            part = pl.ds(pl.multiple_of(j * piece, piece), piece)
            return remote(half_out.at[part], half_in.at[part], half_send, half_recv.at[j], sibling)

        def gather_half(i):
            j = 1 - i
            here = pl.ds(pl.multiple_of(j * piece, piece), piece)
            there = pl.ds(pl.multiple_of(half + j * piece, piece), piece)
            half_out[here, :] = jnp.dot(
                hot_dst[there, :], msg[...], preferred_element_type=jnp.float32
            ).astype(jnp.bfloat16)
            half_copy(j).start()

        loop(0, 2, gather_half)

    with jax.named_scope("sums_rest"):
        def gather_kept(i):
            here = pl.ds(pl.multiple_of(i * piece, piece), piece)
            kept[here, :] = jnp.dot(hot_dst[here, :], msg[...], preferred_element_type=jnp.float32)

        loop(0, 2, gather_kept)

    with jax.named_scope("cot_third"):
        cot_bytes(2 * near, cz_send, cz_recv.at[0]).wait_recv()
        loop(0, near, lambda j: send_cot(j, 1, relay_send, relay_recv.at[0], peer(0, -1)))

    with jax.named_scope("cot_far"):
        cot_bytes(n_z - near, cot_send, cot_recv.at[1]).wait_recv()
        loop(near, n_z, second_far)

    with jax.named_scope("sums_both"):
        order = tuple(range(across, n_x)) + tuple(range(across - 1, -1, -1))
        slot = 0
        for k in order:
            part = slice(k * slab, (k + 1) * slab)
            if k == across:
                half_copy(1).wait_recv()
            if k == across - 1:
                half_copy(0).wait_recv()
            total = kept[part, :] + half_in[part, :].astype(jnp.float32)
            if k == across:
                far[...] = total[:rows]
                b_out[...] = total[rows:].astype(jnp.bfloat16).reshape(n_z - 1, rows, feat)
                far_first(
                    n_z,
                    lambda z: remote(
                        b_out.at[z - 1], b_in.at[z - 1], b_send, b_recv.at[0], peer(z, 0)
                    ).start(),
                )
            elif k:
                x_out[slot] = total.astype(jnp.bfloat16)
                remote(x_out.at[slot], x_in.at[slot], x_send, x_recv.at[0], peer(0, k)).start()
                slot += 1
            else:
                own[...] = total

    with jax.named_scope("cot_rest"):
        loop(near, n_z, lambda j: to_sibling(j, 0))
        loop(0, near, pass_beside)
        cot_bytes(near, relay_send, relay_recv.at[0]).wait_recv()
        loop(0, near, lambda j: to_sibling(j, across))

    with jax.named_scope("cot_rest_far"):
        cot_bytes((n_x - 1) * (n_z - near), cz_send, cz_recv.at[1]).wait_recv()

        def pass_far(j):
            for k in (across, 1, -1):
                to_sibling(j, k)

        loop(near, n_z, pass_far)

    with jax.named_scope("sums_x"):
        if n_x > 2:
            all_of(x_in, x_send, x_recv).wait_recv()
        summed = own[...]
        for k in range(n_x - 2):
            summed = summed + x_in[k].astype(jnp.float32)
        own[...] = summed
        z_out[...] = summed[rows:].astype(jnp.bfloat16).reshape(n_z - 1, rows, feat)
        far_first(
            n_z,
            lambda z: remote(
                z_out.at[z - 1], z_in.at[z - 1], z_send, z_recv.at[0], peer(z, 0)
            ).start(),
        )

    with jax.named_scope("cot_last"):
        all_of(cot.at[:, 0], cc_send, cc_recv).wait_recv()

    with jax.named_scope("backward"):
        for i in range(blocks):
            here = slice(i * width, (i + 1) * width)
            first = jnp.minimum(offsets[i] >> 5, last_window)
            window = cot[pl.ds(first, WINDOW // (CORES * rows))].reshape(WINDOW, feat)
            msg[here, :] = jnp.dot(
                hot_win[here, :], window, preferred_element_type=jnp.float32
            ).astype(jnp.bfloat16)

    with jax.named_scope("d_pre"):
        wide = min(512, edges)
        for i in range(edges // wide):
            here = slice(i * wide, (i + 1) * wide)
            d_hidden = lax.dot_general(
                msg[here, :], wout[...], NT, preferred_element_type=jnp.float32
            )
            hidden[here, :] = (d_hidden * pre[here, :]).astype(jnp.bfloat16)

    with jax.named_scope("source_sums"):
        high, low = split_bf16(
            jnp.dot(hot_src_t[...], hidden[...], preferred_element_type=jnp.float32)
        )
        sums = lax.dot_general(
            high, wnode[...], NT, preferred_element_type=jnp.float32
        ) + lax.dot_general(low, wnode[...], NT, preferred_element_type=jnp.float32)
        node_own = sums[:rows]
        s_out[...] = sums[rows:].astype(jnp.bfloat16).reshape(n_src - 1, rows, feat)
        far_first(
            n_src,
            lambda k: remote(
                s_out.at[k - 1], s_in.at[k - 1], s_send, s_recv.at[0], y_peer(k)
            ).start(),
        )

    with jax.named_scope("sums_far"):
        all_of(b_in, b_send, b_recv).wait_recv()
        far_out[...] = (far[...] + jnp.sum(b_in[...].astype(jnp.float32), axis=0)).astype(jnp.bfloat16)
        far_copy = remote(far_out, far_in, far_send, far_recv.at[0], peer(0, across))
        far_copy.start()

    with jax.named_scope("attr_grads"):
        for i in range(edges // wide):
            here = slice(i * wide, (i + 1) * wide)
            attr_grad[here, :] = lax.dot_general(
                hidden[here, :], wedge[...], NT, preferred_element_type=jnp.float32
            ).astype(jnp.bfloat16)
        attr_store = pltpu.make_async_copy(attr_grad, attr_out, store_sem.at[0])
        attr_store.start()

    with jax.named_scope("drain"):
        all_of(group.at[pl.ds(0, n_src - 1)], feat_send, feat_recv).wait_send()
        cot_bytes(n_z - 1, cot_send, cot_recv.at[0]).wait_send()
        cot_bytes(2 * near + (n_x - 1) * (n_z - near), cz_send, cz_recv.at[0]).wait_send()
        cot_bytes(near, relay_send, relay_recv.at[0]).wait_send()
        all_of(cot.at[:, 0], cc_send, cc_recv).wait_send()
        all_of(half_out, half_send, half_recv).wait_send()
        if n_x > 2:
            all_of(x_out, x_send, x_recv).wait_send()
        all_of(b_out, b_send, b_recv).wait_send()

    with jax.named_scope("last_z"):
        all_of(z_in, z_send, z_recv).wait_recv()
        partial = own[0:rows, :] + jnp.sum(z_in[...].astype(jnp.float32), axis=0)

    with jax.named_scope("last_far"):
        far_copy.wait_recv()
        agg[...] = (partial + far_in[...].astype(jnp.float32)).astype(jnp.bfloat16)
        agg_store = pltpu.make_async_copy(agg, agg_out, store_sem.at[1])
        agg_store.start()

    with jax.named_scope("last_y"):
        all_of(s_in, s_send, s_recv).wait_recv()
        node[...] = (node_own + jnp.sum(s_in[...].astype(jnp.float32), axis=0)).astype(jnp.bfloat16)
        node_store = pltpu.make_async_copy(node, node_out, store_sem.at[2])
        node_store.start()

    with jax.named_scope("drain_last"):
        all_of(z_out, z_send, z_recv).wait_send()
        far_copy.wait_send()
        all_of(s_out, s_send, s_recv).wait_send()
        attr_store.wait()
        agg_store.wait()
        node_store.wait()


def write(*refs):
    count = len(refs) // 2
    sem = refs[-1]
    copies = [
        pltpu.make_async_copy(refs[i], refs[count + i], sem.at[i]) for i in range(count)
    ]
    for copy in copies:
        copy.start()
    for copy in copies:
        copy.wait()


def local(
    n_src, n_x, n_z,
    node_feats, cotangent, edge_attr, src_ids, dst_rel, offsets, counts, w_node, w_edge, bias, w_out,
):
    rows, feat = node_feats.shape
    edges, attr_width = edge_attr.shape
    blocks = offsets.shape[0]
    width = edges // blocks
    hidden = w_node.shape[1]
    slab = rows * n_z
    half = slab * n_x
    f32, bf16 = jnp.float32, jnp.bfloat16
    vmem, dma = pltpu.VMEM, pltpu.SemaphoreType.DMA
    anywhere = pl.BlockSpec(memory_space=pl.ANY)
    operands = (
        node_feats, cotangent, edge_attr,
        src_ids.reshape(blocks, width), dst_rel.reshape(blocks, width), offsets, counts,
        w_node, w_edge, bias.reshape(1, hidden), w_out,
    )
    outs = (
        jax.ShapeDtypeStruct((rows, feat), bf16),
        jax.ShapeDtypeStruct((rows, feat), bf16),
        jax.ShapeDtypeStruct((edges, attr_width), bf16),
    )
    results = pl.pallas_call(
        functools.partial(kernel, (n_src, n_x, n_z, rows)),
        out_shape=outs,
        in_specs=[anywhere] * len(operands),
        out_specs=(anywhere,) * 3,
        scratch_shapes=[
            pltpu.SMEM((blocks,), jnp.int32),
            pltpu.SMEM((blocks,), jnp.int32),
            vmem((n_src, rows, feat), bf16),
            vmem((n_z * n_x, CORES, rows, feat), bf16),
            vmem((edges, attr_width), bf16),
            vmem((blocks, width), jnp.int32),
            vmem((blocks, width), jnp.int32),
            vmem(w_node.shape, bf16),
            vmem(w_edge.shape, bf16),
            vmem((1, hidden), f32),
            vmem(w_out.shape, bf16),
            vmem((edges, 2 * width), bf16),
            vmem((n_src * rows, edges), bf16),
            vmem((CORES * half, edges), bf16),
            vmem((edges, WINDOW), bf16),
            vmem((2 * width, hidden), bf16),
            vmem((edges, hidden), f32),
            vmem((edges, feat), bf16),
            vmem((edges, hidden), bf16),
            vmem((edges, attr_width), bf16),
            vmem((half, feat), bf16),
            vmem((half, feat), bf16),
            vmem((half, feat), f32),
            vmem((slab, feat), f32),
            vmem((rows, feat), f32),
            vmem((max(n_x - 2, 1), slab, feat), bf16),
            vmem((max(n_x - 2, 1), slab, feat), bf16),
            vmem((n_z - 1, rows, feat), bf16),
            vmem((n_z - 1, rows, feat), bf16),
            vmem((rows, feat), bf16),
            vmem((rows, feat), bf16),
            vmem((n_z - 1, rows, feat), bf16),
            vmem((n_z - 1, rows, feat), bf16),
            vmem((n_src - 1, rows, feat), bf16),
            vmem((n_src - 1, rows, feat), bf16),
            vmem((rows, feat), bf16),
            vmem((rows, feat), bf16),
            dma((len(operands),)),
            dma((n_x,)),
            dma((3,)),
            dma((2,)),
            dma((2,)),
        ]
        + [dma((1,))] * 19,
        compiler_params=pltpu.CompilerParams(
            collective_id=0, has_side_effects=True, vmem_limit_bytes=32 * 1024 * 1024
        ),
    )(*(pltpu.with_memory_space_constraint(operand, pltpu.HBM) for operand in operands))
    return pl.pallas_call(
        write,
        out_shape=outs,
        in_specs=[anywhere] * 3,
        out_specs=(anywhere,) * 3,
        scratch_shapes=[dma((3,))],
    )(*(pltpu.with_memory_space_constraint(result, pltpu.VMEM) for result in results))


def build(mesh, n_x):
    n_src, n_dst = mesh.shape["src"], mesh.shape["dst"]
    in_specs = (
        P(("dst", "src"), None),
        P(("src", "dst"), None),
        P(("src", "dst"), None),
        P(("src", "dst")),
        P(("src", "dst")),
        P(("src", "dst")),
        P(("src", "dst")),
        P(),
        P(),
        P(),
        P(),
    )
    out_specs = (P(("src", "dst"), None), P(("dst", "src"), None), P(("src", "dst"), None))
    return jax.shard_map(
        functools.partial(local, n_src, n_x, n_dst // (n_x * CORES)),
        mesh=mesh, in_specs=in_specs, out_specs=out_specs, check_vma=False,
    )


def solution(mesh):
    return build(mesh, X_CHIPS)
```

```python
import functools

import jax
import jax.numpy as jnp
from jax import lax
from jax.experimental import pallas as pl
from jax.experimental.pallas import tpu as pltpu
from jax.sharding import PartitionSpec as P

MESH = pl.DeviceIdType.MESH
X_CHIPS = 4
CORES = 2
WINDOW = 256
NT = (((1,), (1,)), ((), ()))


def split_bf16(value):
    high = value.astype(jnp.bfloat16)
    low = (value - high.astype(jnp.float32)).astype(jnp.bfloat16)
    return high, low


def loop(first, last, step, unroll=1):
    def body(k, carry):
        step(k)
        return carry

    lax.fori_loop(first, last, body, 0, unroll=unroll)


def far_first(size, step, first=0, last=None):
    def body(i):
        step(size // 2 + (1 - 2 * lax.rem(i, 2)) * lax.div(i + 1, 2))

    loop(first, size - 1 if last is None else last, body)


def kernel(
    dims,
    feats_in, cot_in, attr_in, src_in, rel_in, offsets_in, counts_in, wnode_in, wedge_in, bias_in,
    wout_in,
    agg_out, node_out, attr_out,
    offsets, counts, group, cot, attr, src, rel, wnode, wedge, bias, wout,
    hot_src, hot_src_t, hot_dst, hot_win,
    proj, pre, msg, hidden, attr_grad,
    half_out, half_in, kept, own, x_out, x_in, b_out, b_in, far_out, far_in, z_out, z_in, s_out, s_in,
    agg, node,
    load_sem, half_recv, store_sem, cot_recv, cz_recv,
    feat_send, feat_recv, cot_send, cz_send, relay_send, relay_recv, cc_send, cc_recv, half_send,
    x_send, x_recv, b_send, b_recv, far_send, far_recv, z_send, z_recv, s_send, s_recv,
):
    n_src, n_x, n_z, rows = dims
    blocks, width = src.shape
    edges = blocks * width
    feat = group.shape[2]
    me_s = lax.axis_index("src")
    me_d = lax.axis_index("dst")
    me_c = lax.rem(me_d, CORES)
    me_x = lax.rem(lax.div(me_d, CORES), n_x)
    me_z = lax.div(me_d, CORES * n_x)
    slab = rows * n_z
    half = slab * n_x
    across = n_x // 2
    reach = n_z // 4
    near = 2 * reach + 1

    def dst_at(z, x, c):
        return (z * n_x + x) * CORES + c

    def y_peer(k):
        return (lax.rem(me_s + k + n_src, n_src), me_d)

    def peer(z, x):
        return (
            me_s, dst_at(lax.rem(me_z + z + n_z, n_z), lax.rem(me_x + x + n_x, n_x), me_c),
        )

    sibling = (me_s, dst_at(me_z, me_x, 1 - me_c))

    def remote(source, target, send, recv, device):
        return pltpu.make_async_remote_copy(
            src_ref=source, dst_ref=target, send_sem=send.at[0], recv_sem=recv,
            device_id=device, device_id_type=MESH,
        )

    def all_of(ref, send, recv):
        return remote(ref, ref, send, recv.at[0], sibling)


    with jax.named_scope("load"):
        loads = [
            pltpu.make_async_copy(source, target, load_sem.at[i])
            for i, (source, target) in enumerate(
                (
                    (src_in, src), (rel_in, rel), (offsets_in, offsets), (counts_in, counts),
                    (feats_in, group.at[me_s]), (cot_in, cot.at[me_z * n_x + me_x, me_c]),
                    (attr_in, attr), (wedge_in, wedge), (bias_in, bias),
                    (wnode_in, wnode), (wout_in, wout),
                )
            )
        ]
        for load in loads:
            load.start()

    with jax.named_scope("greet"):
        barrier = pltpu.get_barrier_semaphore()

        def greet(device):
            pl.semaphore_signal(barrier, inc=1, device_id=device, device_id_type=MESH)

        far_first(n_src, lambda k: greet(y_peer(k)))
        for k in range(reach, 0, -1):
            greet(peer(k, 0))
            greet(peer(-k, 0))
        for k in range(1, n_x):
            greet(peer(0, k))
        greet(sibling)

    with jax.named_scope("marks_first"):
        for i in range(4):
            loads[i].wait()
        lane = lax.broadcasted_iota(jnp.int32, (width, width), 1)
        sub = lax.broadcasted_iota(jnp.int32, (width, width), 0)
        tall = lax.broadcasted_iota(jnp.int32, (CORES * half, width), 0)
        one_lane = lax.broadcasted_iota(jnp.int32, (1, width), 1)
        last_window = cot.shape[0] - WINDOW // (CORES * rows)

        def hot(mask):
            return jnp.where(mask, 1.0, 0.0).astype(jnp.bfloat16)

        def mark(b):
            here = pl.ds(pl.multiple_of(b * width, width), width)
            ids = src[pl.ds(b, 1), :]
            picked = hot(jnp.broadcast_to(ids, (width, width)).T == lane)
            hot_src[here, 0:width] = picked
            hot_src[here, width : 2 * width] = picked
            owner = lax.rem((ids >> 4) + (n_src - me_s), n_src)
            hot_src_t[:, here] = hot(sub[: n_src * rows] == owner * rows + (ids & (rows - 1)))
            valid = one_lane < counts[b]
            start = offsets[b]
            target = rel[pl.ds(b, 1), :] + start
            owner = target >> 4
            core = lax.rem(owner + me_c, CORES)
            x = lax.rem((owner >> 1) + (n_x - me_x), n_x)
            z = lax.rem(lax.div(owner, CORES * n_x) + (n_z - me_z), n_z)
            place = ((core * n_x + x) * n_z + z) * rows + (target & (rows - 1))
            hot_dst[:, here] = hot(tall == jnp.where(valid, place, -1))
            base = jnp.minimum(start >> 5, last_window) * (CORES * rows)
            inside = jnp.broadcast_to(jnp.where(valid, target - base, -1), (width, width)).T
            hot_win[here, 0:width] = 0.5 * hot(inside == lane)
            hot_win[here, width : 2 * width] = 0.5 * hot(inside == lane + width)

        loop(0, blocks // 4, mark)

    with jax.named_scope("barrier"):
        loads[4].wait()
        loads[5].wait()
        pl.semaphore_wait(barrier, (n_src - 1) + 2 * reach + (n_x - 1) + 1)

    with jax.named_scope("first_sends"):
        def cot_at(j, x):
            z = lax.rem(me_z + (n_z - reach) + j, n_z)
            return cot.at[z * n_x + lax.rem(me_x + x + n_x, n_x), me_c]

        def send_cot(j, x, send, recv, device):
            remote(cot_at(j, x), cot_at(j, x), send, recv, device).start()

        def cot_bytes(count, send, recv):
            return remote(cot.at[pl.ds(0, count), 0], cot.at[pl.ds(0, count), 0], send, recv, sibling)

        def to_sibling(j, x):
            send_cot(j, x, cc_send, cc_recv.at[0], sibling)

        for k in range(reach, 0, -1):
            send_cot(reach, 0, cot_send, cot_recv.at[0], peer(k, 0))
            send_cot(reach, 0, cot_send, cot_recv.at[0], peer(-k, 0))
        mine = group.at[me_s]
        far_first(
            n_src, lambda k: remote(mine, mine, feat_send, feat_recv.at[0], y_peer(k)).start()
        )

        def second(j):
            send_cot(j, 0, cz_send, cz_recv.at[0], peer(0, 1))
            send_cot(j, 0, cz_send, cz_recv.at[0], peer(0, -1))

        def second_far(j):
            for k in (across, 1, -1):
                send_cot(j, 0, cz_send, cz_recv.at[1], peer(0, k))

        def pass_beside(j):
            to_sibling(j, -1)
            to_sibling(j, 1)

    with jax.named_scope("marks"):
        loop(blocks // 4, blocks, mark)

    with jax.named_scope("attr_part"):
        for i in (6, 7, 8):
            loads[i].wait()
        tile = min(256, edges)

        def attr_part(i):
            here = pl.ds(pl.multiple_of(i * tile, tile), tile)
            pre[here, :] = 0.5 * (
                jnp.dot(attr[here, :], wedge[...], preferred_element_type=jnp.float32) + bias[...]
            )

        loop(0, edges // tile, attr_part, True)

    with jax.named_scope("cot_near"):
        cot_bytes(near - 1, cot_send, cot_recv.at[0]).wait_recv()
        for o in range(reach, 0, -1):
            send_cot(reach + o, 0, cot_send, cot_recv.at[1], peer(-reach, 0))
        for o in range(n_z - 3 * reach - 1, 0, -1):
            send_cot(reach - o, 0, cot_send, cot_recv.at[1], peer(reach, 0))
        loop(0, near, second)

    with jax.named_scope("feats_wait"):
        loads[9].wait()
        loads[10].wait()
        all_of(group.at[pl.ds(0, n_src - 1)], feat_send, feat_recv).wait_recv()

    with jax.named_scope("forward"):
        high, low = split_bf16(
            0.5
            * jnp.dot(
                group[...].reshape(n_src * rows, feat), wnode[...], preferred_element_type=jnp.float32
            )
        )
        if n_src * rows < width:
            proj[...] = jnp.zeros_like(proj)
        proj[0 : n_src * rows, :] = high
        proj[width : width + n_src * rows, :] = low

        def activate(i):
            here = slice(i * tile, (i + 1) * tile)
            value = pre[here, :] + jnp.dot(
                hot_src[here, :], proj[...], preferred_element_type=jnp.float32
            )
            rise = 1.0 + jnp.tanh(value)
            silu = value * rise
            hidden[here, :] = silu.astype(jnp.bfloat16)
            pre[here, :] = rise + silu * (2.0 - rise)

        def project(i):
            here = slice(i * tile, (i + 1) * tile)
            msg[here, :] = jnp.dot(
                hidden[here, :], wout[...], preferred_element_type=jnp.float32
            ).astype(jnp.bfloat16)

        tiles = edges // tile
        activate(0)
        for i in range(1, tiles):
            activate(i)
            project(i - 1)
        project(tiles - 1)

    with jax.named_scope("sums"):
        piece = half // 2

        def half_copy(j):
            part = pl.ds(pl.multiple_of(j * piece, piece), piece)
            return remote(half_out.at[part], half_in.at[part], half_send, half_recv.at[j], sibling)

        def gather_half(i):
            j = 1 - i
            here = pl.ds(pl.multiple_of(j * piece, piece), piece)
            there = pl.ds(pl.multiple_of(half + j * piece, piece), piece)
            half_out[here, :] = jnp.dot(
                hot_dst[there, :], msg[...], preferred_element_type=jnp.float32
            ).astype(jnp.bfloat16)
            half_copy(j).start()

        loop(0, 2, gather_half)

    with jax.named_scope("cot_third"):
        cot_bytes(2 * near, cz_send, cz_recv.at[0]).wait_recv()
        loop(0, near, lambda j: send_cot(j, 1, relay_send, relay_recv.at[0], peer(0, -1)))

    with jax.named_scope("cot_far"):
        cot_bytes(n_z - near, cot_send, cot_recv.at[1]).wait_recv()
        loop(near, n_z, second_far)

    with jax.named_scope("sums_rest"):
        def gather_kept(i):
            j = 1 - i
            here = pl.ds(pl.multiple_of(j * piece, piece), piece)
            total = jnp.dot(hot_dst[here, :], msg[...], preferred_element_type=jnp.float32)
            half_copy(j).wait_recv()
            total = total + half_in[here, :].astype(jnp.float32)
            kept[j] = total[:slab]
            x_out[j] = total[slab:].astype(jnp.bfloat16)
            remote(
                x_out.at[j], x_in.at[j], x_send, x_recv.at[0], peer(0, 2 * j + 1)
            ).start()

        loop(0, 2, gather_kept)

    with jax.named_scope("sums_both"):
        b_out[...] = kept[1, rows:, :].astype(jnp.bfloat16).reshape(n_z - 1, rows, feat)
        far_first(
            n_z,
            lambda z: remote(
                b_out.at[z - 1], b_in.at[z - 1], b_send, b_recv.at[0], peer(z, 0)
            ).start(),
        )

    with jax.named_scope("cot_rest"):
        loop(0, n_z, lambda j: to_sibling(j, 0))
        loop(0, near, pass_beside)
        cot_bytes(near, relay_send, relay_recv.at[0]).wait_recv()
        loop(0, near, lambda j: to_sibling(j, across))

    with jax.named_scope("cot_rest_far"):
        cot_bytes((n_x - 1) * (n_z - near), cz_send, cz_recv.at[1]).wait_recv()

        def pass_far(j):
            for k in (across, 1, -1):
                to_sibling(j, k)

        loop(near, n_z, pass_far)

    with jax.named_scope("sums_x"):
        if n_x > 2:
            all_of(x_in, x_send, x_recv).wait_recv()
        summed = kept[0]
        for k in range(n_x - 2):
            summed = summed + x_in[k].astype(jnp.float32)
        own[...] = summed
        z_out[...] = summed[rows:].astype(jnp.bfloat16).reshape(n_z - 1, rows, feat)
        far_first(
            n_z,
            lambda z: remote(
                z_out.at[z - 1], z_in.at[z - 1], z_send, z_recv.at[0], peer(z, 0)
            ).start(),
        )

    with jax.named_scope("cot_last"):
        all_of(cot.at[:, 0], cc_send, cc_recv).wait_recv()

    with jax.named_scope("backward"):
        for i in range(blocks):
            here = slice(i * width, (i + 1) * width)
            first = jnp.minimum(offsets[i] >> 5, last_window)
            window = cot[pl.ds(first, WINDOW // (CORES * rows))].reshape(WINDOW, feat)
            msg[here, :] = jnp.dot(
                hot_win[here, :], window, preferred_element_type=jnp.float32
            ).astype(jnp.bfloat16)

    with jax.named_scope("d_pre"):
        wide = min(512, edges)
        for i in range(edges // wide):
            here = slice(i * wide, (i + 1) * wide)
            d_hidden = lax.dot_general(
                msg[here, :], wout[...], NT, preferred_element_type=jnp.float32
            )
            hidden[here, :] = (d_hidden * pre[here, :]).astype(jnp.bfloat16)

    with jax.named_scope("source_sums"):
        high, low = split_bf16(
            jnp.dot(hot_src_t[...], hidden[...], preferred_element_type=jnp.float32)
        )
        sums = lax.dot_general(
            high, wnode[...], NT, preferred_element_type=jnp.float32
        ) + lax.dot_general(low, wnode[...], NT, preferred_element_type=jnp.float32)
        node_own = sums[:rows]
        s_out[...] = sums[rows:].astype(jnp.bfloat16).reshape(n_src - 1, rows, feat)
        far_first(
            n_src,
            lambda k: remote(
                s_out.at[k - 1], s_in.at[k - 1], s_send, s_recv.at[0], y_peer(k)
            ).start(),
        )

    with jax.named_scope("sums_far"):
        all_of(b_in, b_send, b_recv).wait_recv()
        far_out[...] = (kept[1, :rows, :] + jnp.sum(b_in[...].astype(jnp.float32), axis=0)).astype(jnp.bfloat16)
        far_copy = remote(far_out, far_in, far_send, far_recv.at[0], peer(0, across))
        far_copy.start()

    with jax.named_scope("attr_grads"):
        for i in range(edges // wide):
            here = slice(i * wide, (i + 1) * wide)
            attr_grad[here, :] = lax.dot_general(
                hidden[here, :], wedge[...], NT, preferred_element_type=jnp.float32
            ).astype(jnp.bfloat16)
        attr_store = pltpu.make_async_copy(attr_grad, attr_out, store_sem.at[0])
        attr_store.start()

    with jax.named_scope("drain"):
        all_of(group.at[pl.ds(0, n_src - 1)], feat_send, feat_recv).wait_send()
        cot_bytes(n_z - 1, cot_send, cot_recv.at[0]).wait_send()
        cot_bytes(2 * near + (n_x - 1) * (n_z - near), cz_send, cz_recv.at[0]).wait_send()
        cot_bytes(near, relay_send, relay_recv.at[0]).wait_send()
        all_of(cot.at[:, 0], cc_send, cc_recv).wait_send()
        all_of(half_out, half_send, half_recv).wait_send()
        if n_x > 2:
            all_of(x_out, x_send, x_recv).wait_send()
        all_of(b_out, b_send, b_recv).wait_send()

    with jax.named_scope("last_z"):
        all_of(z_in, z_send, z_recv).wait_recv()
        partial = own[0:rows, :] + jnp.sum(z_in[...].astype(jnp.float32), axis=0)

    with jax.named_scope("last_far"):
        far_copy.wait_recv()
        agg[...] = (partial + far_in[...].astype(jnp.float32)).astype(jnp.bfloat16)
        agg_store = pltpu.make_async_copy(agg, agg_out, store_sem.at[1])
        agg_store.start()

    with jax.named_scope("last_y"):
        all_of(s_in, s_send, s_recv).wait_recv()
        node[...] = (node_own + jnp.sum(s_in[...].astype(jnp.float32), axis=0)).astype(jnp.bfloat16)
        node_store = pltpu.make_async_copy(node, node_out, store_sem.at[2])
        node_store.start()

    with jax.named_scope("drain_last"):
        all_of(z_out, z_send, z_recv).wait_send()
        far_copy.wait_send()
        all_of(s_out, s_send, s_recv).wait_send()
        attr_store.wait()
        agg_store.wait()
        node_store.wait()


def write(*refs):
    count = len(refs) // 2
    sem = refs[-1]
    copies = [
        pltpu.make_async_copy(refs[i], refs[count + i], sem.at[i]) for i in range(count)
    ]
    for copy in copies:
        copy.start()
    for copy in copies:
        copy.wait()


def local(
    n_src, n_x, n_z,
    node_feats, cotangent, edge_attr, src_ids, dst_rel, offsets, counts, w_node, w_edge, bias, w_out,
):
    rows, feat = node_feats.shape
    edges, attr_width = edge_attr.shape
    blocks = offsets.shape[0]
    width = edges // blocks
    hidden = w_node.shape[1]
    slab = rows * n_z
    half = slab * n_x
    f32, bf16 = jnp.float32, jnp.bfloat16
    vmem, dma = pltpu.VMEM, pltpu.SemaphoreType.DMA
    anywhere = pl.BlockSpec(memory_space=pl.ANY)
    operands = (
        node_feats, cotangent, edge_attr,
        src_ids.reshape(blocks, width), dst_rel.reshape(blocks, width), offsets, counts,
        w_node, w_edge, bias.reshape(1, hidden), w_out,
    )
    outs = (
        jax.ShapeDtypeStruct((rows, feat), bf16),
        jax.ShapeDtypeStruct((rows, feat), bf16),
        jax.ShapeDtypeStruct((edges, attr_width), bf16),
    )
    results = pl.pallas_call(
        functools.partial(kernel, (n_src, n_x, n_z, rows)),
        out_shape=outs,
        in_specs=[anywhere] * len(operands),
        out_specs=(anywhere,) * 3,
        scratch_shapes=[
            pltpu.SMEM((blocks,), jnp.int32),
            pltpu.SMEM((blocks,), jnp.int32),
            vmem((n_src, rows, feat), bf16),
            vmem((n_z * n_x, CORES, rows, feat), bf16),
            vmem((edges, attr_width), bf16),
            vmem((blocks, width), jnp.int32),
            vmem((blocks, width), jnp.int32),
            vmem(w_node.shape, bf16),
            vmem(w_edge.shape, bf16),
            vmem((1, hidden), f32),
            vmem(w_out.shape, bf16),
            vmem((edges, 2 * width), bf16),
            vmem((n_src * rows, edges), bf16),
            vmem((CORES * half, edges), bf16),
            vmem((edges, WINDOW), bf16),
            vmem((2 * width, hidden), bf16),
            vmem((edges, hidden), f32),
            vmem((edges, feat), bf16),
            vmem((edges, hidden), bf16),
            vmem((edges, attr_width), bf16),
            vmem((half, feat), bf16),
            vmem((half, feat), bf16),
            vmem((2, slab, feat), f32),
            vmem((slab, feat), f32),
            vmem((max(n_x - 2, 1), slab, feat), bf16),
            vmem((max(n_x - 2, 1), slab, feat), bf16),
            vmem((n_z - 1, rows, feat), bf16),
            vmem((n_z - 1, rows, feat), bf16),
            vmem((rows, feat), bf16),
            vmem((rows, feat), bf16),
            vmem((n_z - 1, rows, feat), bf16),
            vmem((n_z - 1, rows, feat), bf16),
            vmem((n_src - 1, rows, feat), bf16),
            vmem((n_src - 1, rows, feat), bf16),
            vmem((rows, feat), bf16),
            vmem((rows, feat), bf16),
            dma((len(operands),)),
            dma((n_x,)),
            dma((3,)),
            dma((2,)),
            dma((2,)),
        ]
        + [dma((1,))] * 19,
        compiler_params=pltpu.CompilerParams(
            collective_id=0, has_side_effects=True, vmem_limit_bytes=32 * 1024 * 1024
        ),
    )(*(pltpu.with_memory_space_constraint(operand, pltpu.HBM) for operand in operands))
    return pl.pallas_call(
        write,
        out_shape=outs,
        in_specs=[anywhere] * 3,
        out_specs=(anywhere,) * 3,
        scratch_shapes=[dma((3,))],
    )(*(pltpu.with_memory_space_constraint(result, pltpu.VMEM) for result in results))


def build(mesh, n_x):
    n_src, n_dst = mesh.shape["src"], mesh.shape["dst"]
    in_specs = (
        P(("dst", "src"), None),
        P(("src", "dst"), None),
        P(("src", "dst"), None),
        P(("src", "dst")),
        P(("src", "dst")),
        P(("src", "dst")),
        P(("src", "dst")),
        P(),
        P(),
        P(),
        P(),
    )
    out_specs = (P(("src", "dst"), None), P(("dst", "src"), None), P(("src", "dst"), None))
    return jax.shard_map(
        functools.partial(local, n_src, n_x, n_dst // (n_x * CORES)),
        mesh=mesh, in_specs=in_specs, out_specs=out_specs, check_vma=False,
    )


def solution(mesh):
    return build(mesh, X_CHIPS)
```

```python
import functools

import jax
import jax.numpy as jnp
from jax import lax
from jax.experimental import pallas as pl
from jax.experimental.pallas import tpu as pltpu
from jax.sharding import PartitionSpec as P

MESH = pl.DeviceIdType.MESH
X_CHIPS = 4
CORES = 2
WINDOW = 256
NT = (((1,), (1,)), ((), ()))


def split_bf16(value):
    high = value.astype(jnp.bfloat16)
    low = (value - high.astype(jnp.float32)).astype(jnp.bfloat16)
    return high, low


def loop(first, last, step, unroll=1):
    def body(k, carry):
        step(k)
        return carry

    lax.fori_loop(first, last, body, 0, unroll=unroll)


def far_first(size, step, first=0, last=None):
    def body(i):
        step(size // 2 + (1 - 2 * lax.rem(i, 2)) * lax.div(i + 1, 2))

    loop(first, size - 1 if last is None else last, body)


def kernel(
    dims,
    feats_in, cot_in, attr_in, src_in, rel_in, offsets_in, counts_in, wnode_in, wedge_in, bias_in,
    wout_in,
    agg_out, node_out, attr_out,
    offsets, counts, group, cot, attr, src, rel, wnode, wedge, bias, wout,
    hot_src, hot_src_t, hot_dst, hot_win,
    proj, pre, msg, hidden, attr_grad,
    half_out, half_in, kept, own, x_out, x_in, b_out, b_in, far_out, far_in, z_out, z_in, s_out, s_in,
    agg, node,
    load_sem, half_recv, store_sem, cot_recv, cz_recv,
    feat_send, feat_recv, cot_send, cz_send, relay_send, relay_recv, cc_send, cc_recv, half_send,
    x_send, x_recv, b_send, b_recv, far_send, far_recv, z_send, z_recv, s_send, s_recv,
):
    n_src, n_x, n_z, rows = dims
    blocks, width = src.shape
    edges = blocks * width
    feat = group.shape[2]
    me_s = lax.axis_index("src")
    me_d = lax.axis_index("dst")
    me_c = lax.rem(me_d, CORES)
    me_x = lax.rem(lax.div(me_d, CORES), n_x)
    me_z = lax.div(me_d, CORES * n_x)
    slab = rows * n_z
    half = slab * n_x
    across = n_x // 2
    reach = n_z // 4
    near = 2 * reach + 1

    def dst_at(z, x, c):
        return (z * n_x + x) * CORES + c

    def y_peer(k):
        return (lax.rem(me_s + k + n_src, n_src), me_d)

    def peer(z, x):
        return (
            me_s, dst_at(lax.rem(me_z + z + n_z, n_z), lax.rem(me_x + x + n_x, n_x), me_c),
        )

    sibling = (me_s, dst_at(me_z, me_x, 1 - me_c))

    def remote(source, target, send, recv, device):
        return pltpu.make_async_remote_copy(
            src_ref=source, dst_ref=target, send_sem=send.at[0], recv_sem=recv,
            device_id=device, device_id_type=MESH,
        )

    def all_of(ref, send, recv):
        return remote(ref, ref, send, recv.at[0], sibling)


    with jax.named_scope("load"):
        loads = [
            pltpu.make_async_copy(source, target, load_sem.at[i])
            for i, (source, target) in enumerate(
                (
                    (src_in, src), (rel_in, rel), (offsets_in, offsets), (counts_in, counts),
                    (feats_in, group.at[me_s]), (cot_in, cot.at[me_z * n_x + me_x, me_c]),
                    (attr_in, attr), (wedge_in, wedge), (bias_in, bias),
                    (wnode_in, wnode), (wout_in, wout),
                )
            )
        ]
        for load in loads:
            load.start()

    with jax.named_scope("greet"):
        barrier = pltpu.get_barrier_semaphore()

        def greet(device):
            pl.semaphore_signal(barrier, inc=1, device_id=device, device_id_type=MESH)

        far_first(n_src, lambda k: greet(y_peer(k)))
        for k in range(reach, 0, -1):
            greet(peer(k, 0))
            greet(peer(-k, 0))
        for k in range(1, n_x):
            greet(peer(0, k))
        greet(sibling)

    with jax.named_scope("marks_first"):
        for i in range(4):
            loads[i].wait()
        lane = lax.broadcasted_iota(jnp.int32, (width, width), 1)
        sub = lax.broadcasted_iota(jnp.int32, (width, width), 0)
        tall = lax.broadcasted_iota(jnp.int32, (CORES * half, width), 0)
        one_lane = lax.broadcasted_iota(jnp.int32, (1, width), 1)
        last_window = cot.shape[0] - WINDOW // (CORES * rows)

        def hot(mask):
            return jnp.where(mask, 1.0, 0.0).astype(jnp.bfloat16)

        def mark(b):
            here = pl.ds(pl.multiple_of(b * width, width), width)
            ids = src[pl.ds(b, 1), :]
            picked = hot(jnp.broadcast_to(ids, (width, width)).T == lane)
            hot_src[here, 0:width] = picked
            hot_src[here, width : 2 * width] = picked
            owner = lax.rem((ids >> 4) + (n_src - me_s), n_src)
            hot_src_t[:, here] = hot(sub[: n_src * rows] == owner * rows + (ids & (rows - 1)))
            valid = one_lane < counts[b]
            start = offsets[b]
            target = rel[pl.ds(b, 1), :] + start
            owner = target >> 4
            core = lax.rem(owner + me_c, CORES)
            x = lax.rem((owner >> 1) + (n_x - me_x), n_x)
            z = lax.rem(lax.div(owner, CORES * n_x) + (n_z - me_z), n_z)
            place = ((core * n_x + x) * n_z + z) * rows + (target & (rows - 1))
            hot_dst[:, here] = hot(tall == jnp.where(valid, place, -1))
            base = jnp.minimum(start >> 5, last_window) * (CORES * rows)
            inside = jnp.broadcast_to(jnp.where(valid, target - base, -1), (width, width)).T
            hot_win[here, 0:width] = 0.5 * hot(inside == lane)
            hot_win[here, width : 2 * width] = 0.5 * hot(inside == lane + width)

        mark(0)

    with jax.named_scope("barrier"):
        loads[4].wait()
        loads[5].wait()
        pl.semaphore_wait(barrier, (n_src - 1) + 2 * reach + (n_x - 1) + 1)

    with jax.named_scope("first_sends"):
        def cot_at(j, x):
            z = lax.rem(me_z + (n_z - reach) + j, n_z)
            return cot.at[z * n_x + lax.rem(me_x + x + n_x, n_x), me_c]

        def send_cot(j, x, send, recv, device):
            remote(cot_at(j, x), cot_at(j, x), send, recv, device).start()

        def cot_bytes(count, send, recv):
            return remote(cot.at[pl.ds(0, count), 0], cot.at[pl.ds(0, count), 0], send, recv, sibling)

        def to_sibling(j, x):
            send_cot(j, x, cc_send, cc_recv.at[0], sibling)

        for k in range(reach, 0, -1):
            send_cot(reach, 0, cot_send, cot_recv.at[0], peer(k, 0))
            send_cot(reach, 0, cot_send, cot_recv.at[0], peer(-k, 0))
        mine = group.at[me_s]
        far_first(
            n_src, lambda k: remote(mine, mine, feat_send, feat_recv.at[0], y_peer(k)).start()
        )

        def second(j):
            send_cot(j, 0, cz_send, cz_recv.at[0], peer(0, 1))
            send_cot(j, 0, cz_send, cz_recv.at[0], peer(0, -1))

        def second_far(j):
            for k in (across, 1, -1):
                send_cot(j, 0, cz_send, cz_recv.at[1], peer(0, k))

        def pass_beside(j):
            to_sibling(j, -1)
            to_sibling(j, 1)

    with jax.named_scope("marks"):
        loop(1, blocks, mark)

    with jax.named_scope("attr_part"):
        for i in (6, 7, 8):
            loads[i].wait()
        tile = min(256, edges)

        def attr_part(i):
            here = pl.ds(pl.multiple_of(i * tile, tile), tile)
            pre[here, :] = 0.5 * (
                jnp.dot(attr[here, :], wedge[...], preferred_element_type=jnp.float32) + bias[...]
            )

        loop(0, edges // tile, attr_part, True)

    with jax.named_scope("cot_near"):
        cot_bytes(near - 1, cot_send, cot_recv.at[0]).wait_recv()
        for o in range(reach, 0, -1):
            send_cot(reach + o, 0, cot_send, cot_recv.at[1], peer(-reach, 0))
        for o in range(n_z - 3 * reach - 1, 0, -1):
            send_cot(reach - o, 0, cot_send, cot_recv.at[1], peer(reach, 0))
        loop(0, near, second)

    with jax.named_scope("feats_wait"):
        loads[9].wait()
        loads[10].wait()
        all_of(group.at[pl.ds(0, n_src - 1)], feat_send, feat_recv).wait_recv()

    with jax.named_scope("forward"):
        high, low = split_bf16(
            0.5
            * jnp.dot(
                group[...].reshape(n_src * rows, feat), wnode[...], preferred_element_type=jnp.float32
            )
        )
        if n_src * rows < width:
            proj[...] = jnp.zeros_like(proj)
        proj[0 : n_src * rows, :] = high
        proj[width : width + n_src * rows, :] = low

        def activate(i):
            here = slice(i * tile, (i + 1) * tile)
            value = pre[here, :] + jnp.dot(
                hot_src[here, :], proj[...], preferred_element_type=jnp.float32
            )
            rise = 1.0 + jnp.tanh(value)
            silu = value * rise
            hidden[here, :] = silu.astype(jnp.bfloat16)
            pre[here, :] = rise + silu * (2.0 - rise)

        def project(i):
            here = slice(i * tile, (i + 1) * tile)
            msg[here, :] = jnp.dot(
                hidden[here, :], wout[...], preferred_element_type=jnp.float32
            ).astype(jnp.bfloat16)

        tiles = edges // tile
        activate(0)
        for i in range(1, tiles):
            activate(i)
            project(i - 1)
        project(tiles - 1)

    with jax.named_scope("sums"):
        piece = half // 2

        def half_copy(j):
            part = pl.ds(pl.multiple_of(j * piece, piece), piece)
            return remote(half_out.at[part], half_in.at[part], half_send, half_recv.at[j], sibling)

        def gather_half(i):
            j = 1 - i
            here = pl.ds(pl.multiple_of(j * piece, piece), piece)
            there = pl.ds(pl.multiple_of(half + j * piece, piece), piece)
            half_out[here, :] = jnp.dot(
                hot_dst[there, :], msg[...], preferred_element_type=jnp.float32
            ).astype(jnp.bfloat16)
            half_copy(j).start()

        loop(0, 2, gather_half)

    with jax.named_scope("cot_third"):
        cot_bytes(2 * near, cz_send, cz_recv.at[0]).wait_recv()
        loop(0, near, lambda j: send_cot(j, 1, relay_send, relay_recv.at[0], peer(0, -1)))

    with jax.named_scope("cot_far"):
        cot_bytes(n_z - near, cot_send, cot_recv.at[1]).wait_recv()
        loop(near, n_z, second_far)

    with jax.named_scope("sums_rest"):
        def gather_kept(i):
            j = 1 - i
            here = pl.ds(pl.multiple_of(j * piece, piece), piece)
            total = jnp.dot(hot_dst[here, :], msg[...], preferred_element_type=jnp.float32)
            half_copy(j).wait_recv()
            total = total + half_in[here, :].astype(jnp.float32)
            kept[j] = total[:slab]
            x_out[j] = total[slab:].astype(jnp.bfloat16)
            remote(
                x_out.at[j], x_in.at[j], x_send, x_recv.at[0], peer(0, 2 * j + 1)
            ).start()

        loop(0, 2, gather_kept)

    with jax.named_scope("sums_both"):
        b_out[...] = kept[1, rows:, :].astype(jnp.bfloat16).reshape(n_z - 1, rows, feat)
        far_first(
            n_z,
            lambda z: remote(
                b_out.at[z - 1], b_in.at[z - 1], b_send, b_recv.at[0], peer(z, 0)
            ).start(),
        )

    with jax.named_scope("cot_rest"):
        loop(0, n_z, lambda j: to_sibling(j, 0))
        loop(0, near, pass_beside)
        cot_bytes(near, relay_send, relay_recv.at[0]).wait_recv()
        loop(0, near, lambda j: to_sibling(j, across))

    with jax.named_scope("cot_rest_far"):
        cot_bytes((n_x - 1) * (n_z - near), cz_send, cz_recv.at[1]).wait_recv()

        def pass_far(j):
            for k in (across, 1, -1):
                to_sibling(j, k)

        loop(near, n_z, pass_far)

    with jax.named_scope("sums_x"):
        if n_x > 2:
            all_of(x_in, x_send, x_recv).wait_recv()
        summed = kept[0]
        for k in range(n_x - 2):
            summed = summed + x_in[k].astype(jnp.float32)
        own[...] = summed
        z_out[...] = summed[rows:].astype(jnp.bfloat16).reshape(n_z - 1, rows, feat)
        far_first(
            n_z,
            lambda z: remote(
                z_out.at[z - 1], z_in.at[z - 1], z_send, z_recv.at[0], peer(z, 0)
            ).start(),
        )

    with jax.named_scope("cot_last"):
        all_of(cot.at[:, 0], cc_send, cc_recv).wait_recv()

    with jax.named_scope("backward"):
        for i in range(blocks):
            here = slice(i * width, (i + 1) * width)
            first = jnp.minimum(offsets[i] >> 5, last_window)
            window = cot[pl.ds(first, WINDOW // (CORES * rows))].reshape(WINDOW, feat)
            msg[here, :] = jnp.dot(
                hot_win[here, :], window, preferred_element_type=jnp.float32
            ).astype(jnp.bfloat16)

    with jax.named_scope("d_pre"):
        wide = min(512, edges)
        for i in range(edges // wide):
            here = slice(i * wide, (i + 1) * wide)
            d_hidden = lax.dot_general(
                msg[here, :], wout[...], NT, preferred_element_type=jnp.float32
            )
            hidden[here, :] = (d_hidden * pre[here, :]).astype(jnp.bfloat16)

    with jax.named_scope("source_sums"):
        high, low = split_bf16(
            jnp.dot(hot_src_t[...], hidden[...], preferred_element_type=jnp.float32)
        )
        sums = lax.dot_general(
            high, wnode[...], NT, preferred_element_type=jnp.float32
        ) + lax.dot_general(low, wnode[...], NT, preferred_element_type=jnp.float32)
        node_own = sums[:rows]
        s_out[...] = sums[rows:].astype(jnp.bfloat16).reshape(n_src - 1, rows, feat)
        far_first(
            n_src,
            lambda k: remote(
                s_out.at[k - 1], s_in.at[k - 1], s_send, s_recv.at[0], y_peer(k)
            ).start(),
        )

    with jax.named_scope("sums_far"):
        all_of(b_in, b_send, b_recv).wait_recv()
        far_out[...] = (kept[1, :rows, :] + jnp.sum(b_in[...].astype(jnp.float32), axis=0)).astype(jnp.bfloat16)
        far_copy = remote(far_out, far_in, far_send, far_recv.at[0], peer(0, across))
        far_copy.start()

    with jax.named_scope("attr_grads"):
        for i in range(edges // wide):
            here = slice(i * wide, (i + 1) * wide)
            attr_grad[here, :] = lax.dot_general(
                hidden[here, :], wedge[...], NT, preferred_element_type=jnp.float32
            ).astype(jnp.bfloat16)
        attr_store = pltpu.make_async_copy(attr_grad, attr_out, store_sem.at[0])
        attr_store.start()

    with jax.named_scope("drain"):
        all_of(group.at[pl.ds(0, n_src - 1)], feat_send, feat_recv).wait_send()
        cot_bytes(n_z - 1, cot_send, cot_recv.at[0]).wait_send()
        cot_bytes(2 * near + (n_x - 1) * (n_z - near), cz_send, cz_recv.at[0]).wait_send()
        cot_bytes(near, relay_send, relay_recv.at[0]).wait_send()
        all_of(cot.at[:, 0], cc_send, cc_recv).wait_send()
        all_of(half_out, half_send, half_recv).wait_send()
        if n_x > 2:
            all_of(x_out, x_send, x_recv).wait_send()
        all_of(b_out, b_send, b_recv).wait_send()

    with jax.named_scope("last_z"):
        all_of(z_in, z_send, z_recv).wait_recv()
        partial = own[0:rows, :] + jnp.sum(z_in[...].astype(jnp.float32), axis=0)

    with jax.named_scope("last_far"):
        far_copy.wait_recv()
        agg[...] = (partial + far_in[...].astype(jnp.float32)).astype(jnp.bfloat16)
        agg_store = pltpu.make_async_copy(agg, agg_out, store_sem.at[1])
        agg_store.start()

    with jax.named_scope("last_y"):
        all_of(s_in, s_send, s_recv).wait_recv()
        node[...] = (node_own + jnp.sum(s_in[...].astype(jnp.float32), axis=0)).astype(jnp.bfloat16)
        node_store = pltpu.make_async_copy(node, node_out, store_sem.at[2])
        node_store.start()

    with jax.named_scope("drain_last"):
        all_of(z_out, z_send, z_recv).wait_send()
        far_copy.wait_send()
        all_of(s_out, s_send, s_recv).wait_send()
        attr_store.wait()
        agg_store.wait()
        node_store.wait()


def write(*refs):
    count = len(refs) // 2
    sem = refs[-1]
    copies = [
        pltpu.make_async_copy(refs[i], refs[count + i], sem.at[i]) for i in range(count)
    ]
    for copy in copies:
        copy.start()
    for copy in copies:
        copy.wait()


def local(
    n_src, n_x, n_z,
    node_feats, cotangent, edge_attr, src_ids, dst_rel, offsets, counts, w_node, w_edge, bias, w_out,
):
    rows, feat = node_feats.shape
    edges, attr_width = edge_attr.shape
    blocks = offsets.shape[0]
    width = edges // blocks
    hidden = w_node.shape[1]
    slab = rows * n_z
    half = slab * n_x
    f32, bf16 = jnp.float32, jnp.bfloat16
    vmem, dma = pltpu.VMEM, pltpu.SemaphoreType.DMA
    anywhere = pl.BlockSpec(memory_space=pl.ANY)
    operands = (
        node_feats, cotangent, edge_attr,
        src_ids.reshape(blocks, width), dst_rel.reshape(blocks, width), offsets, counts,
        w_node, w_edge, bias.reshape(1, hidden), w_out,
    )
    outs = (
        jax.ShapeDtypeStruct((rows, feat), bf16),
        jax.ShapeDtypeStruct((rows, feat), bf16),
        jax.ShapeDtypeStruct((edges, attr_width), bf16),
    )
    results = pl.pallas_call(
        functools.partial(kernel, (n_src, n_x, n_z, rows)),
        out_shape=outs,
        in_specs=[anywhere] * len(operands),
        out_specs=(anywhere,) * 3,
        scratch_shapes=[
            pltpu.SMEM((blocks,), jnp.int32),
            pltpu.SMEM((blocks,), jnp.int32),
            vmem((n_src, rows, feat), bf16),
            vmem((n_z * n_x, CORES, rows, feat), bf16),
            vmem((edges, attr_width), bf16),
            vmem((blocks, width), jnp.int32),
            vmem((blocks, width), jnp.int32),
            vmem(w_node.shape, bf16),
            vmem(w_edge.shape, bf16),
            vmem((1, hidden), f32),
            vmem(w_out.shape, bf16),
            vmem((edges, 2 * width), bf16),
            vmem((n_src * rows, edges), bf16),
            vmem((CORES * half, edges), bf16),
            vmem((edges, WINDOW), bf16),
            vmem((2 * width, hidden), bf16),
            vmem((edges, hidden), f32),
            vmem((edges, feat), bf16),
            vmem((edges, hidden), bf16),
            vmem((edges, attr_width), bf16),
            vmem((half, feat), bf16),
            vmem((half, feat), bf16),
            vmem((2, slab, feat), f32),
            vmem((slab, feat), f32),
            vmem((max(n_x - 2, 1), slab, feat), bf16),
            vmem((max(n_x - 2, 1), slab, feat), bf16),
            vmem((n_z - 1, rows, feat), bf16),
            vmem((n_z - 1, rows, feat), bf16),
            vmem((rows, feat), bf16),
            vmem((rows, feat), bf16),
            vmem((n_z - 1, rows, feat), bf16),
            vmem((n_z - 1, rows, feat), bf16),
            vmem((n_src - 1, rows, feat), bf16),
            vmem((n_src - 1, rows, feat), bf16),
            vmem((rows, feat), bf16),
            vmem((rows, feat), bf16),
            dma((len(operands),)),
            dma((n_x,)),
            dma((3,)),
            dma((2,)),
            dma((2,)),
        ]
        + [dma((1,))] * 19,
        compiler_params=pltpu.CompilerParams(
            collective_id=0, has_side_effects=True, vmem_limit_bytes=32 * 1024 * 1024
        ),
    )(*(pltpu.with_memory_space_constraint(operand, pltpu.HBM) for operand in operands))
    return pl.pallas_call(
        write,
        out_shape=outs,
        in_specs=[anywhere] * 3,
        out_specs=(anywhere,) * 3,
        scratch_shapes=[dma((3,))],
    )(*(pltpu.with_memory_space_constraint(result, pltpu.VMEM) for result in results))


def build(mesh, n_x):
    n_src, n_dst = mesh.shape["src"], mesh.shape["dst"]
    in_specs = (
        P(("dst", "src"), None),
        P(("src", "dst"), None),
        P(("src", "dst"), None),
        P(("src", "dst")),
        P(("src", "dst")),
        P(("src", "dst")),
        P(("src", "dst")),
        P(),
        P(),
        P(),
        P(),
    )
    out_specs = (P(("src", "dst"), None), P(("dst", "src"), None), P(("src", "dst"), None))
    return jax.shard_map(
        functools.partial(local, n_src, n_x, n_dst // (n_x * CORES)),
        mesh=mesh, in_specs=in_specs, out_specs=out_specs, check_vma=False,
    )


def solution(mesh):
    return build(mesh, X_CHIPS)
```
